32 devices in a mesh: beam: 2 (over y), inp: 8 (over z, x), span: 2 (over core).
Axes of the slice: x: 2, y: 2, z: 4, core: 2. Of those that a mesh axis runs over, the one named last changes fastest.
Arguments:
- voltages: bfloat16 [2, 8, 1024, 16384], P(None, 'beam', 'inp', 'span'), parts along dimension 1, may hold values from -6 to 6
- gains: float32 [2, 8, 1024, 32], P(None, 'beam', 'inp'), parts along dimension 1, may hold values from -4 to 4
Outputs:
- visibilities: bfloat16 [256, 1024, 1024], P(('beam', 'inp'), 'span'), parts along dimension 0
The draws below stay inside these ranges and needn't reach their ends.
There are 2 independent parts, one for each index of `beam`. The reference program is written for one: setup_inputs(seed, part) draws one part's arguments, and reference() takes and returns one part's arrays. A program takes and returns all parts, laid end to end along the dimension named above; each array names one. Nothing has to cross between parts.
All inputs are finite; a program needn't handle non-finite values.
Results may differ from the reference program's by a relative error of at most 0.0085.
Values may be sent and summed in bfloat16 or wider, within the bound.
No kernel may reach another device: no remote copies, remote signals or barrier semaphores. Data moves between devices by JAX's collectives and lax.ppermute only.
A program may use at most 192 MiB of HBM per device.

```python
import math
import jax
import jax.numpy as jnp
from jax import lax

NI = 1024
FINE = 32
TAPS = 4
COARSE = 4
FRAMES = 256
SAMPLES = 8192
SPANS = 2


def shard_levels(own_key, shape, split, low, high):
    def one(dim, shards_of):
        draws = jax.random.uniform(jax.random.fold_in(jax.random.fold_in(own_key, 6), dim), (shards_of,), jnp.float32, low / len(split), high / len(split))
        return jnp.repeat(jnp.exp(draws), shape[dim] // shards_of).reshape((-1,) + (1,) * (len(shape) - dim - 1))

    level = one(*split[0])
    for cut in split[1:]:
        level = level * one(*cut)
    return level


def bell_draw(own_key, extent, spread, most, pieces=(), held_as=jnp.bfloat16):
    values = spread * jax.random.normal(own_key, extent, jnp.float32)
    if pieces:
        values = values * shard_levels(own_key, extent, pieces, -0.22, 0.18)
    return jnp.clip(values, -most, most).astype(held_as)


def setup_inputs(seed: int = 0, part: int = 0) -> dict:
    key_list = jax.random.split(jax.random.key(seed), 3)
    own_keys = jax.random.split(jax.random.fold_in(key_list[2], part), 3)
    return {
        "voltages": bell_draw(own_keys[0], (2, COARSE, NI, SPANS * SAMPLES), 1.0, 6.0, ((2, 8), (3, 2))),
        "gains": bell_draw(own_keys[1], (2, COARSE, NI, FINE), 0.7, 4.0, ((2, 8),), jnp.float32),
    }


def prototype(tap_count, fine_count):
    length = tap_count * fine_count
    offsets = jnp.arange(length).astype(jnp.float32)
    shifted = (offsets - length / 2 + 0.5) / fine_count
    taper = 0.5 - 0.5 * jnp.cos(2.0 * math.pi * (offsets + 0.5) / length)
    window = jnp.sinc(shifted) * taper
    window = window / jnp.sqrt(jnp.sum(window * window))
    return window.reshape(tap_count, fine_count)

def kernels(window, fine_count):
    points = jnp.arange(fine_count)
    phase_steps = points[:, None] * points[None, :] % fine_count
    angles = 2.0 * math.pi * phase_steps.astype(jnp.float32) / fine_count
    cosine = jnp.cos(angles)
    sine_part = jnp.sin(angles)
    result = []
    for tap_index in range(window.shape[0]):
        weights = window[tap_index][:, None]
        hcos = weights * cosine
        hsin = weights * sine_part
        result.append(jnp.stack([jnp.stack([hcos, -hsin]), jnp.stack([hsin, hcos])]))
    return jnp.stack(result)

def reference(voltages, gains):
    window = prototype(TAPS, FINE)
    filters = kernels(window, FINE)
    frame_scale = 1.0 / (SPANS * FRAMES)

    def one_coarse(coarse_args):
        voltage_block, gain_block = coarse_args
        wide = voltage_block.astype(jnp.float32).reshape(2, NI, SPANS, SAMPLES)
        wide = jnp.pad(wide, ((0, 0), (0, 0), (0, 0), (0, (TAPS - 1) * FINE)))
        spectra = jnp.zeros((2, FINE, NI, SPANS, FRAMES), jnp.float32)
        for tap_index in range(TAPS):
            sample_piece = wide[..., tap_index * FINE:tap_index * FINE + SAMPLES]
            sample_piece = sample_piece.reshape(2, NI, SPANS, FRAMES, FINE)
            spectra = spectra + jnp.einsum('aismp,abpk->bkism', sample_piece, filters[tap_index], precision=lax.Precision.HIGHEST)
        gain_real = gain_block[0].T[:, :, None, None]
        gain_imag = gain_block[1].T[:, :, None, None]
        real_part = spectra[0] * gain_real - spectra[1] * gain_imag
        imag_part = spectra[0] * gain_imag + spectra[1] * gain_real
        return jnp.stack([real_part, imag_part]).astype(jnp.bfloat16).reshape(2, FINE, NI, SPANS * FRAMES)
    spectra_all = lax.map(one_coarse, (jnp.moveaxis(voltages, 1, 0), jnp.moveaxis(gains, 1, 0)))
    channel_data = jnp.moveaxis(spectra_all, 1, 2).reshape(COARSE * FINE, 2, NI, SPANS * FRAMES)
    row_index = jnp.arange(NI)
    upper = row_index[:, None] <= row_index[None, :]

    def one_channel(channel_spec):
        left_rows = jnp.concatenate([channel_spec[0], channel_spec[1]], axis=-1)
        right_rows = jnp.concatenate([channel_spec[1], -channel_spec[0]], axis=-1)
        real_sums = jnp.dot(left_rows, left_rows.T, preferred_element_type=jnp.float32)
        imag_sums = jnp.dot(right_rows, left_rows.T, preferred_element_type=jnp.float32)
        return jnp.where(upper, real_sums * frame_scale, imag_sums * frame_scale).astype(jnp.bfloat16)
    return lax.map(one_channel, channel_data)
```

```python
import functools
import math

import jax
import jax.numpy as jnp
import ml_dtypes
import numpy as np
from jax import lax
from jax.experimental import pallas as pl
from jax.experimental.pallas import tpu as pltpu
from jax.sharding import PartitionSpec as P

FINE = 32
TAPS = 4
LANES = 128
GROUP = 8
VMEM = 48 * 1024 * 1024


def prototype(tap_count, fine_count):
    length = tap_count * fine_count
    offsets = jnp.arange(length).astype(jnp.float32)
    shifted = (offsets - length / 2 + 0.5) / fine_count
    taper = 0.5 - 0.5 * jnp.cos(2.0 * math.pi * (offsets + 0.5) / length)
    window = jnp.sinc(shifted) * taper
    window = window / jnp.sqrt(jnp.sum(window * window))
    return window.reshape(tap_count, fine_count)


def kernels(window, fine_count):
    points = jnp.arange(fine_count)
    phase_steps = points[:, None] * points[None, :] % fine_count
    angles = 2.0 * math.pi * phase_steps.astype(jnp.float32) / fine_count
    cosine = jnp.cos(angles)
    sine_part = jnp.sin(angles)
    result = []
    for tap_index in range(window.shape[0]):
        weights = window[tap_index][:, None]
        hcos = weights * cosine
        hsin = weights * sine_part
        result.append(jnp.stack([jnp.stack([hcos, -hsin]), jnp.stack([hsin, hcos])]))
    return jnp.stack(result)


def packed_rows(left_rows, right_rows, left_all, row_start):
    real_sums = jnp.einsum("cif,cjf->cij", left_rows, left_all, preferred_element_type=jnp.float32)
    imag_sums = jnp.einsum("cif,cjf->cij", right_rows, left_all, preferred_element_type=jnp.float32)
    row_index = row_start + jnp.arange(left_rows.shape[1])
    col_index = jnp.arange(left_all.shape[1])
    upper = row_index[:, None] <= col_index[None, :]
    return jnp.where(upper[None], real_sums, imag_sums)


def local_plain(voltages, gains):
    coarse = voltages.shape[1]
    local_inputs = voltages.shape[2]
    samples = voltages.shape[3]
    frames = samples // FINE
    window = prototype(TAPS, FINE)
    filters = kernels(window, FINE)
    filter_table = jnp.transpose(filters, (1, 0, 3, 2, 4))
    filter_high = filter_table.astype(jnp.bfloat16)
    filter_low = (filter_table - filter_high.astype(jnp.float32)).astype(jnp.bfloat16)
    padded = jnp.pad(voltages, ((0, 0), (0, 0), (0, 0), (0, (TAPS - 1) * FINE)))
    stacked = jnp.stack(
        [padded[..., tap_index * FINE : tap_index * FINE + samples] for tap_index in range(TAPS)],
        axis=1,
    )
    stacked = stacked.reshape(2, TAPS, coarse, local_inputs, frames, FINE)
    spectra = jnp.einsum(
        "atcnmp,atpbk->bcknm", stacked, filter_high, preferred_element_type=jnp.float32
    )
    spectra = spectra + jnp.einsum(
        "atcnmp,atpbk->bcknm", stacked, filter_low, preferred_element_type=jnp.float32
    )
    gain_real = jnp.swapaxes(gains[0], 1, 2)[:, :, :, None]
    gain_imag = jnp.swapaxes(gains[1], 1, 2)[:, :, :, None]
    real_part = spectra[0] * gain_real - spectra[1] * gain_imag
    imag_part = spectra[0] * gain_imag + spectra[1] * gain_real
    outgoing = jnp.stack([real_part, imag_part]).astype(jnp.bfloat16)
    outgoing = outgoing.reshape(2, coarse * FINE, local_inputs, frames)
    turned = lax.all_to_all(outgoing, "inp", split_axis=1, concat_axis=2, tiled=True)
    inputs = turned.shape[2]
    span_count = lax.axis_size("span")
    row_count = inputs // span_count
    frame_scale = 1.0 / (span_count * frames)
    row_start = lax.axis_index("span") * row_count
    frame_piece = lax.all_gather(turned, "span", axis=3, tiled=True)
    left_all = jnp.concatenate([frame_piece[0], frame_piece[1]], axis=-1)
    own_rows = lax.dynamic_slice_in_dim(frame_piece, row_start, row_count, 2)
    left_rows = jnp.concatenate([own_rows[0], own_rows[1]], axis=-1)
    right_rows = jnp.concatenate([own_rows[1], -own_rows[0]], axis=-1)
    summed = packed_rows(left_rows, right_rows, left_all, row_start) * frame_scale
    return summed.astype(jnp.bfloat16)


def filter_rows(halves):
    length = TAPS * FINE
    run = -(-(GROUP * FINE + length - FINE) // LANES) * LANES
    offsets = np.arange(length)
    window = np.sinc((offsets - length / 2 + 0.5) / FINE)
    window = window * (0.5 - 0.5 * np.cos(2.0 * np.pi * (offsets + 0.5) / length))
    window = window / np.sqrt(np.sum(window * window))
    angles = 2.0 * np.pi * (offsets[None, :] * np.arange(FINE)[:, None] % FINE) / FINE
    hcos = window * np.cos(angles)
    hsin = window * np.sin(angles)
    table = np.zeros((FINE, 2, GROUP, 2, run))
    for frame in range(GROUP):
        at = slice(frame * FINE, frame * FINE + length)
        table[:, 0, frame, 0, at] = hcos
        table[:, 0, frame, 1, at] = hsin
        table[:, 1, frame, 0, at] = -hsin
        table[:, 1, frame, 1, at] = hcos
    return table.reshape(halves, -1, 2 * run).astype(ml_dtypes.bfloat16)


def filter_kernel(halves, chunks, where_ref, now_ref, next_ref, gain_ref, *rest):
    table_refs = rest[:halves]
    outs = rest[halves:-2]
    turned_ref, wide_ref = rest[-2:]
    step = pl.program_id(0)
    inputs, samples = now_ref.shape[2], now_ref.shape[3]
    per_half = FINE // halves
    run = table_refs[0].shape[2] // 2
    pair = 2 * GROUP

    @pl.when(step == 0)
    def _():
        for part in range(2):
            turned_ref[part] = gain_ref[part, 0].T
            for half in range(halves):
                start = pl.multiple_of(where_ref[1 + half] * per_half, per_half)
                rows = turned_ref[part, pl.ds(start, per_half), :]
                wide_ref[part, half] = jnp.broadcast_to(rows[:, None, :], (per_half, pair, inputs))

    last = step == pl.num_programs(0) - 1
    following = next_ref[:, 0]
    following = jnp.where(last, jnp.zeros_like(following), following)
    table = jnp.concatenate([table_refs[half][0] for half in range(halves)], axis=0)
    for block in range(samples // (pair * FINE)):
        sets = []
        for group in range(2):
            start = (2 * block + group) * GROUP * FINE
            stop = start + run
            columns = []
            for part in range(2):
                columns.append(now_ref[part, 0, :, start : min(stop, samples)])
                if stop > samples:
                    columns.append(following[part, :, : stop - samples])
            sets.append(jnp.concatenate(columns, axis=1))
        lines = jnp.concatenate(sets, axis=0)
        sums = lax.dot_general(
            table, lines, (((1,), (1,)), ((), ())), preferred_element_type=jnp.float32
        )
        sums = sums.reshape(halves, per_half, 2, GROUP, 2 * inputs)
        sums = jnp.concatenate([sums[..., :inputs], sums[..., inputs:]], axis=3)
        frames = slice(block * pair, (block + 1) * pair)
        for half in range(halves):
            raw_real, raw_imag = sums[half, :, 0], sums[half, :, 1]
            gain_real, gain_imag = wide_ref[0, half], wide_ref[1, half]
            real = (raw_real * gain_real - raw_imag * gain_imag).astype(jnp.bfloat16)
            imag = (raw_real * gain_imag + raw_imag * gain_real).astype(jnp.bfloat16)
            start = 0
            for index, count in enumerate(chunks):
                out = outs[half * len(chunks) + index]
                out[:, 0, frames, :] = real[start : start + count]
                out[:, 1, frames, :] = imag[start : start + count]
                start += count


def filter_bank(voltages, gains, tables, where, halves, chunks, samples_step):
    _, _, inputs, samples = voltages.shape
    frames = samples // FINE
    steps = samples // samples_step
    ratio = samples_step // LANES
    frames_step = samples_step // FINE
    _, table_rows, table_columns = tables.shape
    spec = pltpu.PrefetchScalarGridSpec(
        num_scalar_prefetch=1,
        grid=(steps,),
        in_specs=[
            pl.BlockSpec((2, 1, inputs, samples_step), lambda t, w: (0, w[0], 0, t)),
            pl.BlockSpec(
                (2, 1, inputs, LANES),
                lambda t, w: (0, w[0], 0, jnp.minimum((t + 1) * ratio, steps * ratio - 1)),
            ),
            pl.BlockSpec((2, 1, inputs, FINE), lambda t, w: (0, w[0], 0, 0)),
        ]
        + [
            pl.BlockSpec((1, table_rows, table_columns), lambda t, w, half=half: (w[1 + half], 0, 0))
            for half in range(halves)
        ],
        out_specs=[
            pl.BlockSpec((count, 2, frames_step, inputs), lambda t, w: (0, 0, t, 0))
            for _ in range(halves)
            for count in chunks
        ],
        scratch_shapes=[
            pltpu.VMEM((2, FINE, inputs), jnp.float32),
            pltpu.VMEM((2, halves, FINE // halves, 2 * GROUP, inputs), jnp.float32),
        ],
    )
    flops = 2 * 2 * FINE * GROUP * table_columns * inputs * (frames // GROUP)
    outs = pl.pallas_call(
        functools.partial(filter_kernel, halves, chunks),
        out_shape=[
            jax.ShapeDtypeStruct((count, 2, frames, inputs), jnp.bfloat16)
            for _ in range(halves)
            for count in chunks
        ],
        grid_spec=spec,
        compiler_params=pltpu.CompilerParams(vmem_limit_bytes=VMEM),
        cost_estimate=pl.CostEstimate(
            flops=flops, bytes_accessed=16 * inputs * samples, transcendentals=0
        ),
        name="filter_bank",
    )(where, voltages, voltages, gains, *([tables] * halves))
    return [outs[half * len(chunks) : (half + 1) * len(chunks)] for half in range(halves)]


def correlate_kernel(count, spans, tile, scale, where_ref, *rest):
    blocks = rest[: count * spans]
    out_ref, all_ref, rows_ref = rest[-3:]
    _, _, frames, inputs = blocks[0].shape
    total = all_ref.shape[2]
    row_count = out_ref.shape[1]
    depth = spans * 2 * frames
    for span in range(spans):
        for index in range(count):
            start = pl.multiple_of(where_ref[index] * inputs, inputs)
            for part in range(2):
                all_ref[2 * span + part, :, pl.ds(start, inputs)] = blocks[span * count + index][0, part]
    first_row = pl.multiple_of(where_ref[count] * row_count, row_count)
    for start in range(0, row_count, LANES):
        for span in range(spans):
            for part in range(2):
                at = pl.multiple_of(first_row + start, LANES)
                piece = all_ref[2 * span + part, :, pl.ds(at, LANES)].T
                rows = slice(start, start + LANES)
                same = slice((2 * span + part) * frames, (2 * span + part + 1) * frames)
                swap = slice((2 * span + 1 - part) * frames, (2 * span + 2 - part) * frames)
                rows_ref[0, rows, same] = piece
                rows_ref[1, rows, swap] = piece if part == 1 else -piece
    row_tiles, column_tiles = row_count // tile, total // tile

    def one(position, _):
        row, column = position // column_tiles, position % column_tiles
        row_at = pl.multiple_of(row * tile, tile)
        column_at = pl.multiple_of(column * tile, tile)
        row_global = where_ref[count] * row_tiles + row
        columns = all_ref[:, :, pl.ds(column_at, tile)].reshape(depth, tile)

        def product(kind):
            left = rows_ref[kind, pl.ds(row_at, tile), :]
            return jnp.dot(left, columns, preferred_element_type=jnp.float32)

        @pl.when(row_global != column)
        def _():
            kind = jnp.where(column > row_global, 0, 1)
            sums = product(kind) * scale
            out_ref[0, pl.ds(row_at, tile), pl.ds(column_at, tile)] = sums.astype(out_ref.dtype)

        @pl.when(row_global == column)
        def _():
            upper = lax.broadcasted_iota(jnp.int32, (tile, tile), 0) <= lax.broadcasted_iota(
                jnp.int32, (tile, tile), 1
            )
            sums = jnp.where(upper, product(0), product(1)) * scale
            out_ref[0, pl.ds(row_at, tile), pl.ds(column_at, tile)] = sums.astype(out_ref.dtype)

        return 0

    lax.fori_loop(0, row_tiles * column_tiles, one, 0)


def correlate(pieces, where, held, first, channels, row_count, total, tile, scale):
    spans, count = len(pieces), len(pieces[0])
    chunk, _, frames, inputs = pieces[0][0].shape
    depth = spans * 2 * frames
    operands = [piece for row in pieces for piece in row]
    in_specs = [pl.BlockSpec((1, 2, frames, inputs), lambda q, w: (q, 0, 0, 0)) for _ in operands]
    aliases = {}
    if held is not None:
        aliases = {1 + len(operands): 0}
        operands.append(held)
        in_specs.append(pl.BlockSpec(memory_space=pl.ANY))
    return pl.pallas_call(
        functools.partial(correlate_kernel, count, spans, tile, scale),
        out_shape=jax.ShapeDtypeStruct((channels, row_count, total), jnp.bfloat16),
        grid_spec=pltpu.PrefetchScalarGridSpec(
            num_scalar_prefetch=1,
            grid=(chunk,),
            in_specs=in_specs,
            out_specs=pl.BlockSpec((1, row_count, total), lambda q, w: (first + q, 0, 0)),
            scratch_shapes=[
                pltpu.VMEM((2 * spans, frames, total), jnp.bfloat16),
                pltpu.VMEM((2, row_count, depth), jnp.bfloat16),
            ],
        ),
        input_output_aliases=aliases,
        compiler_params=pltpu.CompilerParams(vmem_limit_bytes=VMEM),
        cost_estimate=pl.CostEstimate(
            flops=chunk * 3 * row_count * total * depth,
            bytes_accessed=chunk * 2 * (total * depth + row_count * total),
            transcendentals=0,
        ),
        name="correlate",
    )(where, *operands)


def chunk_sizes(channels):
    sizes, left = [], channels
    while left > 0:
        size = max(1, min(channels // 4, left // 2))
        sizes.append(size)
        left -= size
    return sizes


def local_kernels(count, spans, voltages, gains):
    coarse, inputs, samples = voltages.shape[1:]
    frames = samples // FINE
    halves = count // coarse
    channels = FINE // halves
    chunks = chunk_sizes(channels)
    total = count * inputs
    row_count = total // spans
    tile = min(2 * LANES, row_count)
    here = lax.axis_index("inp")
    span_here = lax.axis_index("span")
    tables = jnp.asarray(filter_rows(halves))
    pair = 2 * GROUP * FINE
    samples_step = 2 * pair if samples % (2 * pair) == 0 else pair
    order = sorted(range(coarse), key=lambda m: -m)
    own = here % halves
    spectra = {}
    for step in order:
        where = jnp.stack([(here // halves) ^ step] + [own ^ half for half in range(halves)])
        banks = filter_bank(
            voltages, gains, tables, where.astype(jnp.int32), halves, chunks, samples_step
        )
        for half in range(halves):
            spectra[step * halves + half] = banks[half]
    places = jnp.stack([here ^ step for step in range(count)] + [span_here]).astype(jnp.int32)
    held, first = None, 0
    for index, size in enumerate(chunks):
        mine = []
        for step in range(count):
            piece = spectra[step][index]
            if step:
                piece = lax.ppermute(piece, "inp", [(i, i ^ step) for i in range(count)])
            mine.append(piece)
        pieces = [mine]
        for other in range(1, spans):
            pieces.append(
                [lax.ppermute(piece, "span", [(i, i ^ other) for i in range(spans)]) for piece in mine]
            )
        held = correlate(
            pieces, places, held, first, channels, row_count, total, tile, 1.0 / (spans * frames)
        )
        first += size
    return held


def power_of_two(number):
    return number > 0 and number & (number - 1) == 0


def solution(mesh):
    count, spans = mesh.shape["inp"], mesh.shape["span"]

    def local(voltages, gains):
        coarse, inputs, samples = voltages.shape[1:]
        fits = (
            power_of_two(count)
            and power_of_two(spans)
            and count % coarse == 0
            and power_of_two(count // coarse)
            and FINE % (count // coarse) == 0
            and (FINE // (count // coarse)) % 8 == 0
            and inputs == LANES
            and samples % (2 * GROUP * FINE) == 0
            and (count * inputs // spans) % (2 * LANES) == 0
        )
        if fits:
            return local_kernels(count, spans, voltages, gains)
        return local_plain(voltages, gains)

    placed = (P(None, "beam", "inp", "span"), P(None, "beam", "inp", None))
    return jax.shard_map(
        local,
        mesh=mesh,
        in_specs=placed,
        out_specs=P(("beam", "inp"), "span", None),
        check_vma=False,
    )
```

```python
import functools
import math

import jax
import jax.numpy as jnp
import ml_dtypes
import numpy as np
from jax import lax
from jax.experimental import pallas as pl
from jax.experimental.pallas import tpu as pltpu
from jax.sharding import PartitionSpec as P

FINE = 32
TAPS = 4
LANES = 128
GROUP = 8
VMEM = 64 * 1024 * 1024 - 64 * 1024
PARTS = (2, 10, 15, 16)


def prototype(tap_count, fine_count):
    length = tap_count * fine_count
    offsets = jnp.arange(length).astype(jnp.float32)
    shifted = (offsets - length / 2 + 0.5) / fine_count
    taper = 0.5 - 0.5 * jnp.cos(2.0 * math.pi * (offsets + 0.5) / length)
    window = jnp.sinc(shifted) * taper
    window = window / jnp.sqrt(jnp.sum(window * window))
    return window.reshape(tap_count, fine_count)


def kernels(window, fine_count):
    points = jnp.arange(fine_count)
    phase_steps = points[:, None] * points[None, :] % fine_count
    angles = 2.0 * math.pi * phase_steps.astype(jnp.float32) / fine_count
    cosine = jnp.cos(angles)
    sine_part = jnp.sin(angles)
    result = []
    for tap_index in range(window.shape[0]):
        weights = window[tap_index][:, None]
        hcos = weights * cosine
        hsin = weights * sine_part
        result.append(jnp.stack([jnp.stack([hcos, -hsin]), jnp.stack([hsin, hcos])]))
    return jnp.stack(result)


def packed_rows(left_rows, right_rows, left_all, row_start):
    real_sums = jnp.einsum("cif,cjf->cij", left_rows, left_all, preferred_element_type=jnp.float32)
    imag_sums = jnp.einsum("cif,cjf->cij", right_rows, left_all, preferred_element_type=jnp.float32)
    row_index = row_start + jnp.arange(left_rows.shape[1])
    col_index = jnp.arange(left_all.shape[1])
    upper = row_index[:, None] <= col_index[None, :]
    return jnp.where(upper[None], real_sums, imag_sums)


def local_plain(voltages, gains):
    coarse = voltages.shape[1]
    local_inputs = voltages.shape[2]
    samples = voltages.shape[3]
    frames = samples // FINE
    window = prototype(TAPS, FINE)
    filters = kernels(window, FINE)
    filter_table = jnp.transpose(filters, (1, 0, 3, 2, 4))
    filter_high = filter_table.astype(jnp.bfloat16)
    filter_low = (filter_table - filter_high.astype(jnp.float32)).astype(jnp.bfloat16)
    padded = jnp.pad(voltages, ((0, 0), (0, 0), (0, 0), (0, (TAPS - 1) * FINE)))
    stacked = jnp.stack(
        [padded[..., tap_index * FINE : tap_index * FINE + samples] for tap_index in range(TAPS)],
        axis=1,
    )
    stacked = stacked.reshape(2, TAPS, coarse, local_inputs, frames, FINE)
    spectra = jnp.einsum(
        "atcnmp,atpbk->bcknm", stacked, filter_high, preferred_element_type=jnp.float32
    )
    spectra = spectra + jnp.einsum(
        "atcnmp,atpbk->bcknm", stacked, filter_low, preferred_element_type=jnp.float32
    )
    gain_real = jnp.swapaxes(gains[0], 1, 2)[:, :, :, None]
    gain_imag = jnp.swapaxes(gains[1], 1, 2)[:, :, :, None]
    real_part = spectra[0] * gain_real - spectra[1] * gain_imag
    imag_part = spectra[0] * gain_imag + spectra[1] * gain_real
    outgoing = jnp.stack([real_part, imag_part]).astype(jnp.bfloat16)
    outgoing = outgoing.reshape(2, coarse * FINE, local_inputs, frames)
    turned = lax.all_to_all(outgoing, "inp", split_axis=1, concat_axis=2, tiled=True)
    inputs = turned.shape[2]
    span_count = lax.axis_size("span")
    row_count = inputs // span_count
    frame_scale = 1.0 / (span_count * frames)
    row_start = lax.axis_index("span") * row_count
    frame_piece = lax.all_gather(turned, "span", axis=3, tiled=True)
    left_all = jnp.concatenate([frame_piece[0], frame_piece[1]], axis=-1)
    own_rows = lax.dynamic_slice_in_dim(frame_piece, row_start, row_count, 2)
    left_rows = jnp.concatenate([own_rows[0], own_rows[1]], axis=-1)
    right_rows = jnp.concatenate([own_rows[1], -own_rows[0]], axis=-1)
    summed = packed_rows(left_rows, right_rows, left_all, row_start) * frame_scale
    return summed.astype(jnp.bfloat16)


def filter_rows(halves, kept):
    length = TAPS * FINE
    run = -(-(GROUP * FINE + length - FINE) // LANES) * LANES
    offsets = np.arange(length)
    window = np.sinc((offsets - length / 2 + 0.5) / FINE)
    window = window * (0.5 - 0.5 * np.cos(2.0 * np.pi * (offsets + 0.5) / length))
    window = window / np.sqrt(np.sum(window * window))
    angles = 2.0 * np.pi * (offsets[None, :] * np.arange(FINE)[:, None] % FINE) / FINE
    hcos = window * np.cos(angles)
    hsin = window * np.sin(angles)
    table = np.zeros((FINE, 2, GROUP, 2, run))
    for frame in range(GROUP):
        at = slice(frame * FINE, frame * FINE + length)
        table[:, 0, frame, 0, at] = hcos
        table[:, 0, frame, 1, at] = hsin
        table[:, 1, frame, 0, at] = -hsin
        table[:, 1, frame, 1, at] = hcos
    table = table.reshape(halves, FINE // halves, -1, 2 * run)[:, kept]
    return table.reshape(-1, 2 * run).astype(ml_dtypes.bfloat16)


def filter_kernel(halves, kept, chunks, now_ref, next_ref, gain_ref, table_ref, *rest):
    outs = rest[:-2]
    turned_ref, wide_ref = rest[-2:]
    step = pl.program_id(1)
    inputs, samples = now_ref.shape[2], now_ref.shape[3]
    per_half = FINE // halves
    count = sum(chunks)
    run = table_ref.shape[1] // 2
    pair = 2 * GROUP

    @pl.when(step == 0)
    def _():
        for part in range(2):
            turned_ref[part] = gain_ref[part, 0].T
            for half in range(halves):
                start = half * per_half + kept.start
                rows = turned_ref[part, start : start + count, :]
                wide_ref[part, half] = jnp.broadcast_to(rows[:, None, :], (count, pair, inputs))

    last = step == pl.num_programs(1) - 1
    following = next_ref[:, 0]
    following = jnp.where(last, jnp.zeros_like(following), following)
    for block in range(samples // (pair * FINE)):
        sets = []
        for group in range(2):
            start = (2 * block + group) * GROUP * FINE
            stop = start + run
            columns = []
            for part in range(2):
                columns.append(now_ref[part, 0, :, start : min(stop, samples)])
                if stop > samples:
                    columns.append(following[part, :, : stop - samples])
            sets.append(jnp.concatenate(columns, axis=1))
        lines = jnp.concatenate(sets, axis=0)
        sums = lax.dot_general(
            table_ref[...], lines, (((1,), (1,)), ((), ())), preferred_element_type=jnp.float32
        )
        sums = sums.reshape(halves, count, 2, GROUP, 2 * inputs)
        sums = jnp.concatenate([sums[..., :inputs], sums[..., inputs:]], axis=3)
        frames = slice(block * pair, (block + 1) * pair)
        for half in range(halves):
            raw_real, raw_imag = sums[half, :, 0], sums[half, :, 1]
            gain_real, gain_imag = wide_ref[0, half], wide_ref[1, half]
            real = (raw_real * gain_real - raw_imag * gain_imag).astype(jnp.bfloat16)
            imag = (raw_real * gain_imag + raw_imag * gain_real).astype(jnp.bfloat16)
            start = 0
            for out, size in zip(outs, chunks):
                out[half, :, 0, frames, :] = real[start : start + size]
                out[half, :, 1, frames, :] = imag[start : start + size]
                start += size


def filter_bank(voltages, gains, halves, first, chunks, samples_step):
    _, coarse, inputs, samples = voltages.shape
    frames = samples // FINE
    steps = samples // samples_step
    ratio = samples_step // LANES
    frames_step = samples_step // FINE
    kept = slice(first, first + sum(chunks))
    table = filter_rows(halves, kept)
    return pl.pallas_call(
        functools.partial(filter_kernel, halves, kept, chunks),
        out_shape=[
            jax.ShapeDtypeStruct((coarse * halves, count, 2, frames, inputs), jnp.bfloat16)
            for count in chunks
        ],
        grid=(coarse, steps),
        in_specs=[
            pl.BlockSpec((2, 1, inputs, samples_step), lambda c, t: (0, c, 0, t)),
            pl.BlockSpec(
                (2, 1, inputs, LANES),
                lambda c, t: (0, c, 0, jnp.minimum((t + 1) * ratio, steps * ratio - 1)),
            ),
            pl.BlockSpec((2, 1, inputs, FINE), lambda c, t: (0, c, 0, 0)),
            pl.BlockSpec(table.shape, lambda c, t: (0, 0)),
        ],
        out_specs=[
            pl.BlockSpec((halves, count, 2, frames_step, inputs), lambda c, t: (c, 0, 0, t, 0))
            for count in chunks
        ],
        scratch_shapes=[
            pltpu.VMEM((2, FINE, inputs), jnp.float32),
            pltpu.VMEM((2, halves, sum(chunks), 2 * GROUP, inputs), jnp.float32),
        ],
        compiler_params=pltpu.CompilerParams(vmem_limit_bytes=VMEM),
        cost_estimate=pl.CostEstimate(flops=4 * table.size * inputs * frames // GROUP * coarse, bytes_accessed=16 * coarse * inputs * samples, transcendentals=0),
        name="filter_bank",
    )(voltages, voltages, gains, jnp.asarray(table))


def gate(released, waits):
    def nothing(*_):
        pass

    anywhere = pl.BlockSpec(memory_space=pl.ANY)
    return pl.pallas_call(
        nothing,
        out_shape=[jax.ShapeDtypeStruct(array.shape, array.dtype) for array in released],
        in_specs=[anywhere] * (len(released) + len(waits)),
        out_specs=[anywhere] * len(released),
        input_output_aliases={index: index for index in range(len(released))},
        compiler_params=pltpu.CompilerParams(vmem_limit_bytes=VMEM),
        cost_estimate=pl.CostEstimate(flops=0, bytes_accessed=0, transcendentals=0),
        name="gate",
    )(*released, *waits)


def correlate_kernel(spans, tile, scale, where_ref, *rest):
    blocks = rest[:spans]
    out_ref, all_ref, rows_ref = rest[-3:]
    count, _, _, frames, inputs = blocks[0].shape
    total = all_ref.shape[2]
    row_count = out_ref.shape[1]
    depth = spans * 2 * frames
    for span in range(spans):
        for index in range(count):
            columns = slice(index * inputs, (index + 1) * inputs)
            for part in range(2):
                all_ref[2 * span + part, :, columns] = blocks[span][index, 0, part]
    first_row = pl.multiple_of(where_ref[0] * row_count, row_count)
    for start in range(0, row_count, LANES):
        for span in range(spans):
            for part in range(2):
                at = pl.multiple_of(first_row + start, LANES)
                piece = all_ref[2 * span + part, :, pl.ds(at, LANES)].T
                rows = slice(start, start + LANES)
                same = slice((2 * span + part) * frames, (2 * span + part + 1) * frames)
                swap = slice((2 * span + 1 - part) * frames, (2 * span + 2 - part) * frames)
                rows_ref[0, rows, same] = piece
                rows_ref[1, rows, swap] = piece if part == 1 else -piece
    row_tiles, column_tiles = row_count // tile, total // tile

    def one(position, _):
        row, column = position // column_tiles, position % column_tiles
        row_at = pl.multiple_of(row * tile, tile)
        column_at = pl.multiple_of(column * tile, tile)
        row_global = where_ref[0] * row_tiles + row
        columns = all_ref[:, :, pl.ds(column_at, tile)].reshape(depth, tile)

        def product(kind):
            left = rows_ref[kind, pl.ds(row_at, tile), :]
            return jnp.dot(left, columns, preferred_element_type=jnp.float32)

        @pl.when(row_global != column)
        def _():
            kind = jnp.where(column > row_global, 0, 1)
            sums = product(kind) * scale
            out_ref[0, pl.ds(row_at, tile), pl.ds(column_at, tile)] = sums.astype(out_ref.dtype)

        @pl.when(row_global == column)
        def _():
            upper = lax.broadcasted_iota(jnp.int32, (tile, tile), 0) <= lax.broadcasted_iota(
                jnp.int32, (tile, tile), 1
            )
            sums = jnp.where(upper, product(0), product(1)) * scale
            out_ref[0, pl.ds(row_at, tile), pl.ds(column_at, tile)] = sums.astype(out_ref.dtype)

        return 0

    lax.fori_loop(0, row_tiles * column_tiles, one, 0)


def correlate(pieces, where, held, first, channels, row_count, total, tile, scale):
    spans = len(pieces)
    count, chunk, _, frames, inputs = pieces[0].shape
    depth = spans * 2 * frames
    operands = list(pieces)
    in_specs = [pl.BlockSpec((count, 1, 2, frames, inputs), lambda q, w: (0, q, 0, 0, 0)) for _ in operands]
    aliases = {}
    if held is not None:
        aliases = {1 + len(operands): 0}
        operands.append(held)
        in_specs.append(pl.BlockSpec(memory_space=pl.ANY))
    return pl.pallas_call(
        functools.partial(correlate_kernel, spans, tile, scale),
        out_shape=jax.ShapeDtypeStruct((channels, row_count, total), jnp.bfloat16),
        grid_spec=pltpu.PrefetchScalarGridSpec(
            num_scalar_prefetch=1,
            grid=(chunk,),
            in_specs=in_specs,
            out_specs=pl.BlockSpec((1, row_count, total), lambda q, w: (first + q, 0, 0)),
            scratch_shapes=[
                pltpu.VMEM((2 * spans, frames, total), jnp.bfloat16),
                pltpu.VMEM((2, row_count, depth), jnp.bfloat16),
            ],
        ),
        input_output_aliases=aliases,
        compiler_params=pltpu.CompilerParams(vmem_limit_bytes=VMEM),
        cost_estimate=pl.CostEstimate(
            flops=chunk * 3 * row_count * total * depth,
            bytes_accessed=chunk * 2 * (total * depth + row_count * total),
            transcendentals=0,
        ),
        name="correlate",
    )(where, *operands)


def chunk_sizes(channels):
    cuts = sorted({0} | {max(1, channels * part // 16) for part in PARTS})
    return [stop - start for start, stop in zip(cuts, cuts[1:])]


def local_kernels(count, spans, voltages, gains):
    coarse, inputs, samples = voltages.shape[1:]
    frames = samples // FINE
    halves = count // coarse
    channels = FINE // halves
    chunks = chunk_sizes(channels)
    total = count * inputs
    row_count = total // spans
    tile = min(2 * LANES, row_count)
    pair = 2 * GROUP * FINE
    samples_step = max(size for size in (pair, 2 * pair, 4 * pair) if samples % size == 0)
    where = jnp.stack([lax.axis_index("span")]).astype(jnp.int32)
    outgoing = list(filter_bank(voltages, gains, halves, 0, chunks[:1], samples_step))
    if len(chunks) > 1:
        outgoing += list(filter_bank(voltages, gains, halves, chunks[0], chunks[1:], samples_step))
    held, first = None, 0
    for index, size in enumerate(chunks):
        turned = lax.all_to_all(outgoing[index], "inp", split_axis=0, concat_axis=0, tiled=True)
        if index > 0:
            turned, held = gate([turned, held], [])
        pieces = [turned]
        for other in range(1, spans):
            pieces.append(lax.ppermute(turned, "span", [(i, i ^ other) for i in range(spans)]))
        held = correlate(
            pieces, where, held, first, channels, row_count, total, tile, 1.0 / (spans * frames)
        )
        first += size
    return held


def power_of_two(number):
    return number > 0 and number & (number - 1) == 0


def solution(mesh):
    count, spans = mesh.shape["inp"], mesh.shape["span"]

    def local(voltages, gains):
        coarse, inputs, samples = voltages.shape[1:]
        fits = (
            power_of_two(count)
            and power_of_two(spans)
            and count % coarse == 0
            and power_of_two(count // coarse)
            and FINE % (count // coarse) == 0
            and (FINE // (count // coarse)) % 8 == 0
            and inputs == LANES
            and samples % (2 * GROUP * FINE) == 0
            and (count * inputs // spans) % (2 * LANES) == 0
        )
        if fits:
            return local_kernels(count, spans, voltages, gains)
        return local_plain(voltages, gains)

    placed = (P(None, "beam", "inp", "span"), P(None, "beam", "inp", None))
    return jax.shard_map(
        local,
        mesh=mesh,
        in_specs=placed,
        out_specs=P(("beam", "inp"), "span", None),
        check_vma=False,
    )
```

```python
import functools
import math

import jax
import jax.numpy as jnp
import ml_dtypes
import numpy as np
from jax import lax
from jax.experimental import pallas as pl
from jax.experimental.pallas import tpu as pltpu
from jax.sharding import PartitionSpec as P

FINE = 32
TAPS = 4
LANES = 128
GROUP = 8
VMEM = 64 * 1024 * 1024 - 64 * 1024
EARLY = 2
PARTS = (10, 15, 16)


def prototype(tap_count, fine_count):
    length = tap_count * fine_count
    offsets = jnp.arange(length).astype(jnp.float32)
    shifted = (offsets - length / 2 + 0.5) / fine_count
    taper = 0.5 - 0.5 * jnp.cos(2.0 * math.pi * (offsets + 0.5) / length)
    window = jnp.sinc(shifted) * taper
    window = window / jnp.sqrt(jnp.sum(window * window))
    return window.reshape(tap_count, fine_count)


def kernels(window, fine_count):
    points = jnp.arange(fine_count)
    phase_steps = points[:, None] * points[None, :] % fine_count
    angles = 2.0 * math.pi * phase_steps.astype(jnp.float32) / fine_count
    cosine = jnp.cos(angles)
    sine_part = jnp.sin(angles)
    result = []
    for tap_index in range(window.shape[0]):
        weights = window[tap_index][:, None]
        hcos = weights * cosine
        hsin = weights * sine_part
        result.append(jnp.stack([jnp.stack([hcos, -hsin]), jnp.stack([hsin, hcos])]))
    return jnp.stack(result)


def packed_rows(left_rows, right_rows, left_all, row_start):
    real_sums = jnp.einsum("cif,cjf->cij", left_rows, left_all, preferred_element_type=jnp.float32)
    imag_sums = jnp.einsum("cif,cjf->cij", right_rows, left_all, preferred_element_type=jnp.float32)
    row_index = row_start + jnp.arange(left_rows.shape[1])
    col_index = jnp.arange(left_all.shape[1])
    upper = row_index[:, None] <= col_index[None, :]
    return jnp.where(upper[None], real_sums, imag_sums)


def local_plain(voltages, gains):
    coarse = voltages.shape[1]
    local_inputs = voltages.shape[2]
    samples = voltages.shape[3]
    frames = samples // FINE
    window = prototype(TAPS, FINE)
    filters = kernels(window, FINE)
    filter_table = jnp.transpose(filters, (1, 0, 3, 2, 4))
    filter_high = filter_table.astype(jnp.bfloat16)
    filter_low = (filter_table - filter_high.astype(jnp.float32)).astype(jnp.bfloat16)
    padded = jnp.pad(voltages, ((0, 0), (0, 0), (0, 0), (0, (TAPS - 1) * FINE)))
    stacked = jnp.stack(
        [padded[..., tap_index * FINE : tap_index * FINE + samples] for tap_index in range(TAPS)],
        axis=1,
    )
    stacked = stacked.reshape(2, TAPS, coarse, local_inputs, frames, FINE)
    spectra = jnp.einsum(
        "atcnmp,atpbk->bcknm", stacked, filter_high, preferred_element_type=jnp.float32
    )
    spectra = spectra + jnp.einsum(
        "atcnmp,atpbk->bcknm", stacked, filter_low, preferred_element_type=jnp.float32
    )
    gain_real = jnp.swapaxes(gains[0], 1, 2)[:, :, :, None]
    gain_imag = jnp.swapaxes(gains[1], 1, 2)[:, :, :, None]
    real_part = spectra[0] * gain_real - spectra[1] * gain_imag
    imag_part = spectra[0] * gain_imag + spectra[1] * gain_real
    outgoing = jnp.stack([real_part, imag_part]).astype(jnp.bfloat16)
    outgoing = outgoing.reshape(2, coarse * FINE, local_inputs, frames)
    turned = lax.all_to_all(outgoing, "inp", split_axis=1, concat_axis=2, tiled=True)
    inputs = turned.shape[2]
    span_count = lax.axis_size("span")
    row_count = inputs // span_count
    frame_scale = 1.0 / (span_count * frames)
    row_start = lax.axis_index("span") * row_count
    frame_piece = lax.all_gather(turned, "span", axis=3, tiled=True)
    left_all = jnp.concatenate([frame_piece[0], frame_piece[1]], axis=-1)
    own_rows = lax.dynamic_slice_in_dim(frame_piece, row_start, row_count, 2)
    left_rows = jnp.concatenate([own_rows[0], own_rows[1]], axis=-1)
    right_rows = jnp.concatenate([own_rows[1], -own_rows[0]], axis=-1)
    summed = packed_rows(left_rows, right_rows, left_all, row_start) * frame_scale
    return summed.astype(jnp.bfloat16)


def filter_rows():
    length = TAPS * FINE
    run = -(-(GROUP * FINE + length - FINE) // LANES) * LANES
    offsets = np.arange(length)
    window = np.sinc((offsets - length / 2 + 0.5) / FINE)
    window = window * (0.5 - 0.5 * np.cos(2.0 * np.pi * (offsets + 0.5) / length))
    window = window / np.sqrt(np.sum(window * window))
    angles = 2.0 * np.pi * (offsets[None, :] * np.arange(FINE)[:, None] % FINE) / FINE
    hcos = window * np.cos(angles)
    hsin = window * np.sin(angles)
    table = np.zeros((FINE, 2, GROUP, 2, run))
    for frame in range(GROUP):
        at = slice(frame * FINE, frame * FINE + length)
        table[:, 0, frame, 0, at] = hcos
        table[:, 0, frame, 1, at] = hsin
        table[:, 1, frame, 0, at] = -hsin
        table[:, 1, frame, 1, at] = hcos
    return table.reshape(-1, 2 * run).astype(ml_dtypes.bfloat16)


def filter_kernel(halves, chunks, lead, pairs, volt_ref, gain_ref, table_ref, *rest):
    outs, wide_ref = rest[-1 - len(chunks) : -1], rest[-1]
    inputs, samples = volt_ref.shape[2], volt_ref.shape[3]
    per_half = FINE // halves
    run = table_ref.shape[1] // 2
    hop = GROUP * FINE
    wide_ref[...] = jnp.broadcast_to(gain_ref[:, 0][:, :, None, :], wide_ref.shape)

    def one(pair, inside):
        sets = []
        for group in range(2):
            start = lead + (2 * pair + group) * hop
            columns = []
            for part in range(2):
                if inside:
                    columns.append(volt_ref[part, 0, :, pl.ds(pl.multiple_of(start, LANES), run)])
                else:
                    stop = min(start + run, samples)
                    columns.append(volt_ref[part, 0, :, start:stop])
                    if start + run > stop:
                        columns.append(jnp.zeros((inputs, start + run - stop), volt_ref.dtype))
            sets.append(jnp.concatenate(columns, axis=1))
        lines = jnp.concatenate(sets, axis=0)
        sums = lax.dot_general(
            table_ref[...], lines, (((1,), (1,)), ((), ())), preferred_element_type=jnp.float32
        )
        sums = sums.reshape(FINE, 2, GROUP, 2 * inputs)
        raw_real = jnp.concatenate([sums[:, 0, :, :inputs], sums[:, 0, :, inputs:]], axis=1)
        raw_imag = jnp.concatenate([sums[:, 1, :, :inputs], sums[:, 1, :, inputs:]], axis=1)
        gain_real, gain_imag = wide_ref[0], wide_ref[1]
        real = (raw_real * gain_real - raw_imag * gain_imag).astype(jnp.bfloat16)
        imag = (raw_real * gain_imag + raw_imag * gain_real).astype(jnp.bfloat16)
        frames = pl.ds(pl.multiple_of(2 * GROUP * pair, 2 * GROUP), 2 * GROUP) if inside else pl.ds(
            2 * GROUP * pair, 2 * GROUP
        )
        for half in range(halves):
            start = half * per_half
            for out, size in zip(outs, chunks):
                out[half, :, 0, frames, :] = real[start : start + size]
                out[half, :, 1, frames, :] = imag[start : start + size]
                start += size

    whole = min(pairs, (samples - lead - run + hop) // (2 * hop))

    def loop(pair, _):
        one(pair, True)
        return 0

    lax.fori_loop(0, whole, loop, 0)
    for pair in range(whole, pairs):
        one(pair, False)


def filter_bank(voltages, gains, halves, chunks, first_frame, last_frame, waits=()):
    _, coarse, inputs, samples = voltages.shape
    table = filter_rows()
    run = table.shape[1] // 2
    frames = last_frame - first_frame
    ahead = run - GROUP * FINE
    block = min(samples, last_frame * FINE + ahead)
    return pl.pallas_call(
        functools.partial(
            filter_kernel, halves, chunks, first_frame * FINE, frames // (2 * GROUP)
        ),
        out_shape=[
            jax.ShapeDtypeStruct((coarse * halves, count, 2, frames, inputs), jnp.bfloat16)
            for count in chunks
        ],
        grid=(coarse,),
        in_specs=[
            pl.BlockSpec((2, 1, inputs, block), lambda c: (0, c, 0, 0)),
            pl.BlockSpec((2, 1, FINE, inputs), lambda c: (0, c, 0, 0)),
            pl.BlockSpec(table.shape, lambda c: (0, 0)),
        ]
        + [pl.BlockSpec(memory_space=pl.ANY)] * len(waits),
        out_specs=[
            pl.BlockSpec((halves, count, 2, frames, inputs), lambda c: (c, 0, 0, 0, 0))
            for count in chunks
        ],
        scratch_shapes=[pltpu.VMEM((2, FINE, 2 * GROUP, inputs), jnp.float32)],
        compiler_params=pltpu.CompilerParams(vmem_limit_bytes=VMEM),
        cost_estimate=pl.CostEstimate(
            flops=4 * table.size * inputs * frames // GROUP * coarse,
            bytes_accessed=16 * coarse * inputs * frames * FINE,
            transcendentals=0,
        ),
        name="filter_bank",
    )(voltages, gains, jnp.asarray(table), *waits)


def gate(released, waits):
    def nothing(*_):
        pass

    anywhere = pl.BlockSpec(memory_space=pl.ANY)
    return pl.pallas_call(
        nothing,
        out_shape=[jax.ShapeDtypeStruct(array.shape, array.dtype) for array in released],
        in_specs=[anywhere] * (len(released) + len(waits)),
        out_specs=[anywhere] * len(released),
        input_output_aliases={index: index for index in range(len(released))},
        compiler_params=pltpu.CompilerParams(vmem_limit_bytes=VMEM),
        cost_estimate=pl.CostEstimate(flops=0, bytes_accessed=0, transcendentals=0),
        name="gate",
    )(*released, *waits)


def correlate_kernel(pieces, tile, scale, where_ref, *rest):
    blocks = rest[:pieces]
    out_ref, rows_ref = rest[-2:]
    inputs = blocks[0].shape[4]
    row_count, total = out_ref.shape[1:]
    depth = rows_ref.shape[2]
    per_tile = tile // inputs
    row_tiles, column_tiles = row_count // tile, total // tile

    def columns_of(position):
        sources = [position * per_tile + index for index in range(per_tile)]
        parts = [
            jnp.concatenate([block[source, 0, part] for source in sources], axis=1)
            for part in range(2)
            for block in blocks
        ]
        return jnp.concatenate(parts, axis=0)

    first_tile = where_ref[0] * row_tiles
    unit = (
        lax.broadcasted_iota(jnp.int32, (tile, tile), 0)
        == lax.broadcasted_iota(jnp.int32, (tile, tile), 1)
    )
    unit = jnp.where(unit, 1.0, 0.0).astype(jnp.bfloat16)
    for row in range(row_tiles):
        at = slice(row * tile, (row + 1) * tile)
        turned = lax.dot_general(
            unit, columns_of(first_tile + row), (((1,), (1,)), ((), ())), preferred_element_type=jnp.float32
        ).astype(jnp.bfloat16)
        rows_ref[0, at, :] = turned
        rows_ref[1, at, : depth // 2] = turned[:, depth // 2 :]
        rows_ref[1, at, depth // 2 :] = -turned[:, : depth // 2]

    def one(column, _):
        right = columns_of(column)
        column_at = pl.ds(pl.multiple_of(column * tile, tile), tile)
        for row in range(row_tiles):
            at = slice(row * tile, (row + 1) * tile)
            global_row = first_tile + row

            @pl.when(global_row != column)
            def _():
                kind = jnp.where(column > global_row, 0, 1)
                sums = jnp.dot(rows_ref[kind, at, :], right, preferred_element_type=jnp.float32) * scale
                out_ref[0, at, column_at] = sums.astype(out_ref.dtype)

            @pl.when(global_row == column)
            def _():
                upper = lax.broadcasted_iota(jnp.int32, (tile, tile), 0) <= lax.broadcasted_iota(
                    jnp.int32, (tile, tile), 1
                )
                real = jnp.dot(rows_ref[0, at, :], right, preferred_element_type=jnp.float32)
                imag = jnp.dot(rows_ref[1, at, :], right, preferred_element_type=jnp.float32)
                out_ref[0, at, column_at] = (jnp.where(upper, real, imag) * scale).astype(out_ref.dtype)

        return 0

    lax.fori_loop(0, column_tiles, one, 0)


def correlate(pieces, where, held, first, count, channels, row_count, total, tile, scale):
    sources, _, _, _, inputs = pieces[0][0].shape
    depth = 2 * sum(array.shape[3] for array, _ in pieces)
    operands = [array for array, _ in pieces]
    in_specs = [
        pl.BlockSpec((sources, 1, 2, array.shape[3], inputs), lambda q, w, start=start: (0, start + q, 0, 0, 0))
        for array, start in pieces
    ]
    aliases = {}
    if held is not None:
        aliases = {1 + len(operands): 0}
        operands.append(held)
        in_specs.append(pl.BlockSpec(memory_space=pl.ANY))
    return pl.pallas_call(
        functools.partial(correlate_kernel, len(pieces), tile, scale),
        out_shape=jax.ShapeDtypeStruct((channels, row_count, total), jnp.bfloat16),
        grid_spec=pltpu.PrefetchScalarGridSpec(
            num_scalar_prefetch=1,
            grid=(count,),
            in_specs=in_specs,
            out_specs=pl.BlockSpec((1, row_count, total), lambda q, w: (first + q, 0, 0)),
            scratch_shapes=[pltpu.VMEM((2, row_count, depth), jnp.bfloat16)],
        ),
        input_output_aliases=aliases,
        compiler_params=pltpu.CompilerParams(vmem_limit_bytes=VMEM),
        cost_estimate=pl.CostEstimate(
            flops=count * 8 * row_count * total * depth,
            bytes_accessed=count * 16 * total * depth,
            transcendentals=0,
        ),
        name="correlate",
    )(where, *operands)


def chunk_sizes(channels):
    cuts = sorted({0} | {max(1, channels * part // 16) for part in PARTS})
    return [stop - start for start, stop in zip(cuts, cuts[1:])]


def local_kernels(count, spans, voltages, gains):
    coarse, inputs, samples = voltages.shape[1:]
    frames = samples // FINE
    halves = count // coarse
    channels = FINE // halves
    chunks = chunk_sizes(channels)
    total = count * inputs
    row_count = total // spans
    early = max(2 * GROUP, frames * EARLY // 16 // (2 * GROUP) * (2 * GROUP))
    scale = 1.0 / (spans * frames)
    where = jnp.stack([lax.axis_index("span")]).astype(jnp.int32)
    gains = jnp.swapaxes(gains, 2, 3)

    def across(array):
        return lax.all_to_all(array, "inp", split_axis=0, concat_axis=0, tiled=True)

    def other_spans(array):
        return [
            lax.ppermute(array, "span", [(i, i ^ other) for i in range(spans)]) for other in range(1, spans)
        ]

    outgoing = filter_bank(voltages, gains, halves, [channels], 0, early)
    outgoing = list(outgoing)
    outgoing += list(filter_bank(voltages, gains, halves, chunks, early, frames, outgoing))
    turned = across(outgoing[0])
    outgoing[1] = gate([outgoing[1]], [turned])[0]
    first_frames = [turned] + other_spans(turned)
    held, first = None, 0
    for index, size in enumerate(chunks):
        turned = across(outgoing[1 + index])
        if held is not None:
            turned, held = gate([turned, held], [])
        pieces = [(array, first) for array in first_frames]
        pieces += [(array, 0) for array in [turned] + other_spans(turned)]
        held = correlate(
            pieces, where, held, first, size, channels, row_count, total, 2 * LANES, scale
        )
        first += size
    return held


def power_of_two(number):
    return number > 0 and number & (number - 1) == 0


def solution(mesh):
    count, spans = mesh.shape["inp"], mesh.shape["span"]

    def local(voltages, gains):
        coarse, inputs, samples = voltages.shape[1:]
        fits = (
            power_of_two(count)
            and power_of_two(spans)
            and count % coarse == 0
            and power_of_two(count // coarse)
            and FINE % (count // coarse) == 0
            and (FINE // (count // coarse)) % 8 == 0
            and inputs == LANES
            and samples % (2 * GROUP * FINE) == 0
            and samples >= 8 * GROUP * FINE
            and (count * inputs // spans) % (2 * LANES) == 0
        )
        if fits:
            return local_kernels(count, spans, voltages, gains)
        return local_plain(voltages, gains)

    placed = (P(None, "beam", "inp", "span"), P(None, "beam", "inp", None))
    return jax.shard_map(
        local,
        mesh=mesh,
        in_specs=placed,
        out_specs=P(("beam", "inp"), "span", None),
        check_vma=False,
    )
```

```python
import functools
import math

import jax
import jax.numpy as jnp
import ml_dtypes
import numpy as np
from jax import lax
from jax.experimental import pallas as pl
from jax.experimental.pallas import tpu as pltpu
from jax.sharding import PartitionSpec as P

FINE = 32
TAPS = 4
LANES = 128
GROUP = 8
VMEM = 64 * 1024 * 1024 - 64 * 1024
UNROLL = 4
EARLY = 1
PARTS = (13, 16)


def prototype(tap_count, fine_count):
    length = tap_count * fine_count
    offsets = jnp.arange(length).astype(jnp.float32)
    shifted = (offsets - length / 2 + 0.5) / fine_count
    taper = 0.5 - 0.5 * jnp.cos(2.0 * math.pi * (offsets + 0.5) / length)
    window = jnp.sinc(shifted) * taper
    window = window / jnp.sqrt(jnp.sum(window * window))
    return window.reshape(tap_count, fine_count)


def kernels(window, fine_count):
    points = jnp.arange(fine_count)
    phase_steps = points[:, None] * points[None, :] % fine_count
    angles = 2.0 * math.pi * phase_steps.astype(jnp.float32) / fine_count
    cosine = jnp.cos(angles)
    sine_part = jnp.sin(angles)
    result = []
    for tap_index in range(window.shape[0]):
        weights = window[tap_index][:, None]
        hcos = weights * cosine
        hsin = weights * sine_part
        result.append(jnp.stack([jnp.stack([hcos, -hsin]), jnp.stack([hsin, hcos])]))
    return jnp.stack(result)


def packed_rows(left_rows, right_rows, left_all, row_start):
    real_sums = jnp.einsum("cif,cjf->cij", left_rows, left_all, preferred_element_type=jnp.float32)
    imag_sums = jnp.einsum("cif,cjf->cij", right_rows, left_all, preferred_element_type=jnp.float32)
    row_index = row_start + jnp.arange(left_rows.shape[1])
    col_index = jnp.arange(left_all.shape[1])
    upper = row_index[:, None] <= col_index[None, :]
    return jnp.where(upper[None], real_sums, imag_sums)


def local_plain(voltages, gains):
    coarse = voltages.shape[1]
    local_inputs = voltages.shape[2]
    samples = voltages.shape[3]
    frames = samples // FINE
    window = prototype(TAPS, FINE)
    filters = kernels(window, FINE)
    filter_table = jnp.transpose(filters, (1, 0, 3, 2, 4))
    filter_high = filter_table.astype(jnp.bfloat16)
    filter_low = (filter_table - filter_high.astype(jnp.float32)).astype(jnp.bfloat16)
    padded = jnp.pad(voltages, ((0, 0), (0, 0), (0, 0), (0, (TAPS - 1) * FINE)))
    stacked = jnp.stack(
        [padded[..., tap_index * FINE : tap_index * FINE + samples] for tap_index in range(TAPS)],
        axis=1,
    )
    stacked = stacked.reshape(2, TAPS, coarse, local_inputs, frames, FINE)
    spectra = jnp.einsum(
        "atcnmp,atpbk->bcknm", stacked, filter_high, preferred_element_type=jnp.float32
    )
    spectra = spectra + jnp.einsum(
        "atcnmp,atpbk->bcknm", stacked, filter_low, preferred_element_type=jnp.float32
    )
    gain_real = jnp.swapaxes(gains[0], 1, 2)[:, :, :, None]
    gain_imag = jnp.swapaxes(gains[1], 1, 2)[:, :, :, None]
    real_part = spectra[0] * gain_real - spectra[1] * gain_imag
    imag_part = spectra[0] * gain_imag + spectra[1] * gain_real
    outgoing = jnp.stack([real_part, imag_part]).astype(jnp.bfloat16)
    outgoing = outgoing.reshape(2, coarse * FINE, local_inputs, frames)
    turned = lax.all_to_all(outgoing, "inp", split_axis=1, concat_axis=2, tiled=True)
    inputs = turned.shape[2]
    span_count = lax.axis_size("span")
    row_count = inputs // span_count
    frame_scale = 1.0 / (span_count * frames)
    row_start = lax.axis_index("span") * row_count
    frame_piece = lax.all_gather(turned, "span", axis=3, tiled=True)
    left_all = jnp.concatenate([frame_piece[0], frame_piece[1]], axis=-1)
    own_rows = lax.dynamic_slice_in_dim(frame_piece, row_start, row_count, 2)
    left_rows = jnp.concatenate([own_rows[0], own_rows[1]], axis=-1)
    right_rows = jnp.concatenate([own_rows[1], -own_rows[0]], axis=-1)
    summed = packed_rows(left_rows, right_rows, left_all, row_start) * frame_scale
    return summed.astype(jnp.bfloat16)


def filter_rows():
    length = TAPS * FINE
    run = -(-(GROUP * FINE + length - FINE) // LANES) * LANES
    offsets = np.arange(length)
    window = np.sinc((offsets - length / 2 + 0.5) / FINE)
    window = window * (0.5 - 0.5 * np.cos(2.0 * np.pi * (offsets + 0.5) / length))
    window = window / np.sqrt(np.sum(window * window))
    angles = 2.0 * np.pi * (offsets[None, :] * np.arange(FINE)[:, None] % FINE) / FINE
    hcos = window * np.cos(angles)
    hsin = window * np.sin(angles)
    table = np.zeros((FINE, 2, GROUP, 2, run))
    for frame in range(GROUP):
        at = slice(frame * FINE, frame * FINE + length)
        table[:, 0, frame, 0, at] = hcos
        table[:, 0, frame, 1, at] = hsin
        table[:, 1, frame, 0, at] = -hsin
        table[:, 1, frame, 1, at] = hcos
    return table.reshape(-1, 2 * run).astype(ml_dtypes.bfloat16)


def filter_kernel(halves, chunks, lead, pairs, volt_ref, gain_ref, table_ref, *rest):
    outs, wide_ref = rest[-1 - len(chunks) : -1], rest[-1]
    inputs, samples = volt_ref.shape[2], volt_ref.shape[3]
    per_half = FINE // halves
    run = table_ref.shape[1] // 2
    hop = GROUP * FINE
    wide_ref[...] = jnp.broadcast_to(gain_ref[:, 0][:, :, None, :], wide_ref.shape)

    def one(pair, inside):
        sets = []
        for group in range(2):
            start = lead + (2 * pair + group) * hop
            columns = []
            for part in range(2):
                if inside:
                    columns.append(volt_ref[part, 0, :, pl.ds(pl.multiple_of(start, LANES), run)])
                else:
                    stop = min(start + run, samples)
                    columns.append(volt_ref[part, 0, :, start:stop])
                    if start + run > stop:
                        columns.append(jnp.zeros((inputs, start + run - stop), volt_ref.dtype))
            sets.append(jnp.concatenate(columns, axis=1))
        lines = jnp.concatenate(sets, axis=0)
        sums = lax.dot_general(
            table_ref[...], lines, (((1,), (1,)), ((), ())), preferred_element_type=jnp.float32
        )
        sums = sums.reshape(FINE, 2, GROUP, 2 * inputs)
        raw_real = jnp.concatenate([sums[:, 0, :, :inputs], sums[:, 0, :, inputs:]], axis=1)
        raw_imag = jnp.concatenate([sums[:, 1, :, :inputs], sums[:, 1, :, inputs:]], axis=1)
        gain_real, gain_imag = wide_ref[0], wide_ref[1]
        real = (raw_real * gain_real - raw_imag * gain_imag).astype(jnp.bfloat16)
        imag = (raw_real * gain_imag + raw_imag * gain_real).astype(jnp.bfloat16)
        frames = pl.ds(pl.multiple_of(2 * GROUP * pair, 2 * GROUP), 2 * GROUP) if inside else pl.ds(
            2 * GROUP * pair, 2 * GROUP
        )
        for half in range(halves):
            start = half * per_half
            for out, size in zip(outs, chunks):
                out[half, :, 0, frames, :] = real[start : start + size]
                out[half, :, 1, frames, :] = imag[start : start + size]
                start += size

    whole = min(pairs, (samples - lead - run + hop) // (2 * hop))

    def loop(pair, _):
        one(pair, True)
        return 0

    lax.fori_loop(0, whole, loop, 0, unroll=UNROLL)
    for pair in range(whole, pairs):
        one(pair, False)


def filter_bank(voltages, gains, halves, chunks, first_frame, last_frame, waits=()):
    _, coarse, inputs, samples = voltages.shape
    table = filter_rows()
    run = table.shape[1] // 2
    frames = last_frame - first_frame
    ahead = run - GROUP * FINE
    block = min(samples, last_frame * FINE + ahead)
    return pl.pallas_call(
        functools.partial(
            filter_kernel, halves, chunks, first_frame * FINE, frames // (2 * GROUP)
        ),
        out_shape=[
            jax.ShapeDtypeStruct((coarse * halves, count, 2, frames, inputs), jnp.bfloat16)
            for count in chunks
        ],
        grid=(coarse,),
        in_specs=[
            pl.BlockSpec((2, 1, inputs, block), lambda c: (0, c, 0, 0)),
            pl.BlockSpec((2, 1, FINE, inputs), lambda c: (0, c, 0, 0)),
            pl.BlockSpec(table.shape, lambda c: (0, 0)),
        ]
        + [pl.BlockSpec(memory_space=pl.ANY)] * len(waits),
        out_specs=[
            pl.BlockSpec((halves, count, 2, frames, inputs), lambda c: (c, 0, 0, 0, 0))
            for count in chunks
        ],
        scratch_shapes=[pltpu.VMEM((2, FINE, 2 * GROUP, inputs), jnp.float32)],
        compiler_params=pltpu.CompilerParams(vmem_limit_bytes=VMEM),
        cost_estimate=pl.CostEstimate(
            flops=4 * table.size * inputs * frames // GROUP * coarse,
            bytes_accessed=16 * coarse * inputs * frames * FINE,
            transcendentals=0,
        ),
        name="filter_bank",
    )(voltages, gains, jnp.asarray(table), *waits)


def gate(released, waits):
    def nothing(*_):
        pass

    anywhere = pl.BlockSpec(memory_space=pl.ANY)
    return pl.pallas_call(
        nothing,
        out_shape=[jax.ShapeDtypeStruct(array.shape, array.dtype) for array in released],
        in_specs=[anywhere] * (len(released) + len(waits)),
        out_specs=[anywhere] * len(released),
        input_output_aliases={index: index for index in range(len(released))},
        compiler_params=pltpu.CompilerParams(vmem_limit_bytes=VMEM),
        cost_estimate=pl.CostEstimate(flops=0, bytes_accessed=0, transcendentals=0),
        name="gate",
    )(*released, *waits)


def correlate_kernel(pieces, tile, scale, where_ref, *rest):
    blocks = rest[:pieces]
    out_ref, rows_ref = rest[-2:]
    inputs = blocks[0].shape[4]
    row_count, total = out_ref.shape[1:]
    depth = rows_ref.shape[1]
    per_tile = tile // inputs
    row_tiles, column_tiles = row_count // tile, total // tile

    def columns_of(position):
        sources = [position * per_tile + index for index in range(per_tile)]
        parts = [
            jnp.concatenate([block[source, 0, part] for source in sources], axis=1)
            for part in range(2)
            for block in blocks
        ]
        return jnp.concatenate(parts, axis=0)

    first_tile = where_ref[0] * row_tiles
    unit = (
        lax.broadcasted_iota(jnp.int32, (tile, tile), 0)
        == lax.broadcasted_iota(jnp.int32, (tile, tile), 1)
    )
    unit = jnp.where(unit, 1.0, 0.0).astype(jnp.bfloat16)
    for row in range(row_tiles):
        turned = lax.dot_general(
            unit, columns_of(first_tile + row), (((1,), (1,)), ((), ())), preferred_element_type=jnp.float32
        ).astype(jnp.bfloat16)
        imag_at = slice(row * tile, (row + 1) * tile)
        real_at = slice(row_count + row * tile, row_count + (row + 1) * tile)
        rows_ref[real_at, :] = turned
        rows_ref[imag_at, : depth // 2] = turned[:, depth // 2 :]
        rows_ref[imag_at, depth // 2 :] = -turned[:, : depth // 2]

    def product(start, size, column):
        left = rows_ref[pl.ds(pl.multiple_of(start, tile), size), :]
        return jnp.dot(left, columns_of(column), preferred_element_type=jnp.float32) * scale

    def outside(index, _):
        column = jnp.where(index < first_tile, index, index + row_tiles)
        column_at = pl.ds(pl.multiple_of(column * tile, tile), tile)
        start = jnp.where(index < first_tile, 0, row_count)
        out_ref[0, :, column_at] = product(start, row_count, column).astype(out_ref.dtype)
        return 0

    lax.fori_loop(0, column_tiles - row_tiles, outside, 0, unroll=True)
    upper = lax.broadcasted_iota(jnp.int32, (tile, tile), 0) <= lax.broadcasted_iota(jnp.int32, (tile, tile), 1)
    column_at = pl.ds(pl.multiple_of(first_tile * tile, tile), tile)
    sums = product(0, 3 * tile, first_tile)
    out_ref[0, :tile, column_at] = jnp.where(upper, sums[2 * tile :], sums[:tile]).astype(out_ref.dtype)
    out_ref[0, tile:, column_at] = sums[tile : 2 * tile].astype(out_ref.dtype)
    column_at = pl.ds(pl.multiple_of((first_tile + 1) * tile, tile), tile)
    sums = product(tile, 3 * tile, first_tile + 1)
    out_ref[0, :tile, column_at] = sums[tile : 2 * tile].astype(out_ref.dtype)
    out_ref[0, tile:, column_at] = jnp.where(upper, sums[2 * tile :], sums[:tile]).astype(out_ref.dtype)


def correlate(pieces, where, held, first, count, channels, row_count, total, tile, scale):
    sources, _, _, _, inputs = pieces[0][0].shape
    depth = 2 * sum(array.shape[3] for array, _ in pieces)
    operands = [array for array, _ in pieces]
    in_specs = [
        pl.BlockSpec((sources, 1, 2, array.shape[3], inputs), lambda q, w, start=start: (0, start + q, 0, 0, 0))
        for array, start in pieces
    ]
    aliases = {}
    if held is not None:
        aliases = {1 + len(operands): 0}
        operands.append(held)
        in_specs.append(pl.BlockSpec(memory_space=pl.ANY))
    return pl.pallas_call(
        functools.partial(correlate_kernel, len(pieces), tile, scale),
        out_shape=jax.ShapeDtypeStruct((channels, row_count, total), jnp.bfloat16),
        grid_spec=pltpu.PrefetchScalarGridSpec(
            num_scalar_prefetch=1,
            grid=(count,),
            in_specs=in_specs,
            out_specs=pl.BlockSpec((1, row_count, total), lambda q, w: (first + q, 0, 0)),
            scratch_shapes=[pltpu.VMEM((2 * row_count, depth), jnp.bfloat16)],
        ),
        input_output_aliases=aliases,
        compiler_params=pltpu.CompilerParams(vmem_limit_bytes=VMEM),
        cost_estimate=pl.CostEstimate(
            flops=count * 8 * row_count * total * depth,
            bytes_accessed=count * 16 * total * depth,
            transcendentals=0,
        ),
        name="correlate",
    )(where, *operands)


def chunk_sizes(channels):
    cuts = sorted({0} | {max(1, channels * part // 16) for part in PARTS})
    return [stop - start for start, stop in zip(cuts, cuts[1:])]


def local_kernels(count, spans, voltages, gains):
    coarse, inputs, samples = voltages.shape[1:]
    frames = samples // FINE
    halves = count // coarse
    channels = FINE // halves
    chunks = chunk_sizes(channels)
    total = count * inputs
    row_count = total // spans
    early = max(2 * GROUP, frames * EARLY // 16 // (2 * GROUP) * (2 * GROUP))
    scale = 1.0 / (spans * frames)
    where = jnp.stack([lax.axis_index("span")]).astype(jnp.int32)
    gains = jnp.swapaxes(gains, 2, 3)

    def across(array):
        return lax.all_to_all(array, "inp", split_axis=0, concat_axis=0, tiled=True)

    def other_spans(array):
        return [
            lax.ppermute(array, "span", [(i, i ^ other) for i in range(spans)]) for other in range(1, spans)
        ]

    outgoing = filter_bank(voltages, gains, halves, [channels], 0, early)
    outgoing = list(outgoing)
    outgoing += list(filter_bank(voltages, gains, halves, chunks, early, frames, outgoing))
    turned = across(outgoing[0])
    outgoing[1] = gate([outgoing[1]], [turned])[0]
    first_frames = [turned] + other_spans(turned)
    held, first = None, 0
    for index, size in enumerate(chunks):
        turned = across(outgoing[1 + index])
        if held is not None:
            turned, held = gate([turned, held], [])
        pieces = [(array, first) for array in first_frames]
        pieces += [(array, 0) for array in [turned] + other_spans(turned)]
        held = correlate(
            pieces, where, held, first, size, channels, row_count, total, 2 * LANES, scale
        )
        first += size
    return held


def power_of_two(number):
    return number > 0 and number & (number - 1) == 0


def solution(mesh):
    count, spans = mesh.shape["inp"], mesh.shape["span"]

    def local(voltages, gains):
        coarse, inputs, samples = voltages.shape[1:]
        fits = (
            power_of_two(count)
            and power_of_two(spans)
            and count % coarse == 0
            and power_of_two(count // coarse)
            and FINE % (count // coarse) == 0
            and (FINE // (count // coarse)) % 8 == 0
            and inputs == LANES
            and samples % (2 * GROUP * FINE) == 0
            and samples >= 8 * GROUP * FINE
            and count * inputs // spans == 4 * LANES
        )
        if fits:
            return local_kernels(count, spans, voltages, gains)
        return local_plain(voltages, gains)

    placed = (P(None, "beam", "inp", "span"), P(None, "beam", "inp", None))
    return jax.shard_map(
        local,
        mesh=mesh,
        in_specs=placed,
        out_specs=P(("beam", "inp"), "span", None),
        check_vma=False,
    )
```

```python
import functools
import math

import jax
import jax.numpy as jnp
import ml_dtypes
import numpy as np
from jax import lax
from jax.experimental import pallas as pl
from jax.experimental.pallas import tpu as pltpu
from jax.sharding import PartitionSpec as P

FINE = 32
TAPS = 4
LANES = 128
GROUP = 8
VMEM = 64 * 1024 * 1024 - 64 * 1024
UNROLL = 4
EARLY = 1
PARTS = (14, 16)


def prototype(tap_count, fine_count):
    length = tap_count * fine_count
    offsets = jnp.arange(length).astype(jnp.float32)
    shifted = (offsets - length / 2 + 0.5) / fine_count
    taper = 0.5 - 0.5 * jnp.cos(2.0 * math.pi * (offsets + 0.5) / length)
    window = jnp.sinc(shifted) * taper
    window = window / jnp.sqrt(jnp.sum(window * window))
    return window.reshape(tap_count, fine_count)


def kernels(window, fine_count):
    points = jnp.arange(fine_count)
    phase_steps = points[:, None] * points[None, :] % fine_count
    angles = 2.0 * math.pi * phase_steps.astype(jnp.float32) / fine_count
    cosine = jnp.cos(angles)
    sine_part = jnp.sin(angles)
    result = []
    for tap_index in range(window.shape[0]):
        weights = window[tap_index][:, None]
        hcos = weights * cosine
        hsin = weights * sine_part
        result.append(jnp.stack([jnp.stack([hcos, -hsin]), jnp.stack([hsin, hcos])]))
    return jnp.stack(result)


def packed_rows(left_rows, right_rows, left_all, row_start):
    real_sums = jnp.einsum("cif,cjf->cij", left_rows, left_all, preferred_element_type=jnp.float32)
    imag_sums = jnp.einsum("cif,cjf->cij", right_rows, left_all, preferred_element_type=jnp.float32)
    row_index = row_start + jnp.arange(left_rows.shape[1])
    col_index = jnp.arange(left_all.shape[1])
    upper = row_index[:, None] <= col_index[None, :]
    return jnp.where(upper[None], real_sums, imag_sums)


def local_plain(voltages, gains):
    coarse = voltages.shape[1]
    local_inputs = voltages.shape[2]
    samples = voltages.shape[3]
    frames = samples // FINE
    window = prototype(TAPS, FINE)
    filters = kernels(window, FINE)
    filter_table = jnp.transpose(filters, (1, 0, 3, 2, 4))
    filter_high = filter_table.astype(jnp.bfloat16)
    filter_low = (filter_table - filter_high.astype(jnp.float32)).astype(jnp.bfloat16)
    padded = jnp.pad(voltages, ((0, 0), (0, 0), (0, 0), (0, (TAPS - 1) * FINE)))
    stacked = jnp.stack(
        [padded[..., tap_index * FINE : tap_index * FINE + samples] for tap_index in range(TAPS)],
        axis=1,
    )
    stacked = stacked.reshape(2, TAPS, coarse, local_inputs, frames, FINE)
    spectra = jnp.einsum(
        "atcnmp,atpbk->bcknm", stacked, filter_high, preferred_element_type=jnp.float32
    )
    spectra = spectra + jnp.einsum(
        "atcnmp,atpbk->bcknm", stacked, filter_low, preferred_element_type=jnp.float32
    )
    gain_real = jnp.swapaxes(gains[0], 1, 2)[:, :, :, None]
    gain_imag = jnp.swapaxes(gains[1], 1, 2)[:, :, :, None]
    real_part = spectra[0] * gain_real - spectra[1] * gain_imag
    imag_part = spectra[0] * gain_imag + spectra[1] * gain_real
    outgoing = jnp.stack([real_part, imag_part]).astype(jnp.bfloat16)
    outgoing = outgoing.reshape(2, coarse * FINE, local_inputs, frames)
    turned = lax.all_to_all(outgoing, "inp", split_axis=1, concat_axis=2, tiled=True)
    inputs = turned.shape[2]
    span_count = lax.axis_size("span")
    row_count = inputs // span_count
    frame_scale = 1.0 / (span_count * frames)
    row_start = lax.axis_index("span") * row_count
    frame_piece = lax.all_gather(turned, "span", axis=3, tiled=True)
    left_all = jnp.concatenate([frame_piece[0], frame_piece[1]], axis=-1)
    own_rows = lax.dynamic_slice_in_dim(frame_piece, row_start, row_count, 2)
    left_rows = jnp.concatenate([own_rows[0], own_rows[1]], axis=-1)
    right_rows = jnp.concatenate([own_rows[1], -own_rows[0]], axis=-1)
    summed = packed_rows(left_rows, right_rows, left_all, row_start) * frame_scale
    return summed.astype(jnp.bfloat16)


def filter_rows():
    length = TAPS * FINE
    run = -(-(GROUP * FINE + length - FINE) // LANES) * LANES
    offsets = np.arange(length)
    window = np.sinc((offsets - length / 2 + 0.5) / FINE)
    window = window * (0.5 - 0.5 * np.cos(2.0 * np.pi * (offsets + 0.5) / length))
    window = window / np.sqrt(np.sum(window * window))
    angles = 2.0 * np.pi * (offsets[None, :] * np.arange(FINE)[:, None] % FINE) / FINE
    hcos = window * np.cos(angles)
    hsin = window * np.sin(angles)
    table = np.zeros((FINE, 2, GROUP, 2, run))
    for frame in range(GROUP):
        at = slice(frame * FINE, frame * FINE + length)
        table[:, 0, frame, 0, at] = hcos
        table[:, 0, frame, 1, at] = hsin
        table[:, 1, frame, 0, at] = -hsin
        table[:, 1, frame, 1, at] = hcos
    return table.reshape(-1, 2 * run).astype(ml_dtypes.bfloat16)


def filter_kernel(halves, chunks, lead, pairs, volt_ref, gain_ref, table_ref, *rest):
    outs, wide_ref = rest[-1 - len(chunks) : -1], rest[-1]
    inputs, samples = volt_ref.shape[2], volt_ref.shape[3]
    per_half = FINE // halves
    run = table_ref.shape[1] // 2
    hop = GROUP * FINE
    wide_ref[...] = jnp.broadcast_to(gain_ref[:, 0][:, :, None, :], wide_ref.shape)

    def one(pair, inside):
        sets = []
        for group in range(2):
            start = lead + (2 * pair + group) * hop
            columns = []
            for part in range(2):
                if inside:
                    columns.append(volt_ref[part, 0, :, pl.ds(pl.multiple_of(start, LANES), run)])
                else:
                    stop = min(start + run, samples)
                    columns.append(volt_ref[part, 0, :, start:stop])
                    if start + run > stop:
                        columns.append(jnp.zeros((inputs, start + run - stop), volt_ref.dtype))
            sets.append(jnp.concatenate(columns, axis=1))
        lines = jnp.concatenate(sets, axis=0)
        sums = lax.dot_general(
            table_ref[...], lines, (((1,), (1,)), ((), ())), preferred_element_type=jnp.float32
        )
        sums = sums.reshape(FINE, 2, GROUP, 2 * inputs)
        raw_real = jnp.concatenate([sums[:, 0, :, :inputs], sums[:, 0, :, inputs:]], axis=1)
        raw_imag = jnp.concatenate([sums[:, 1, :, :inputs], sums[:, 1, :, inputs:]], axis=1)
        gain_real, gain_imag = wide_ref[0], wide_ref[1]
        real = (raw_real * gain_real - raw_imag * gain_imag).astype(jnp.bfloat16)
        imag = (raw_real * gain_imag + raw_imag * gain_real).astype(jnp.bfloat16)
        frames = pl.ds(pl.multiple_of(2 * GROUP * pair, 2 * GROUP), 2 * GROUP) if inside else pl.ds(
            2 * GROUP * pair, 2 * GROUP
        )
        for half in range(halves):
            start = half * per_half
            for out, size in zip(outs, chunks):
                out[half, :, 0, frames, :] = real[start : start + size]
                out[half, :, 1, frames, :] = imag[start : start + size]
                start += size

    whole = min(pairs, (samples - lead - run + hop) // (2 * hop))

    def loop(pair, _):
        one(pair, True)
        return 0

    lax.fori_loop(0, whole, loop, 0, unroll=UNROLL)
    for pair in range(whole, pairs):
        one(pair, False)


def filter_bank(voltages, gains, halves, chunks, first_frame, last_frame, waits=()):
    _, coarse, inputs, samples = voltages.shape
    table = filter_rows()
    run = table.shape[1] // 2
    frames = last_frame - first_frame
    ahead = run - GROUP * FINE
    block = min(samples, last_frame * FINE + ahead)
    return pl.pallas_call(
        functools.partial(
            filter_kernel, halves, chunks, first_frame * FINE, frames // (2 * GROUP)
        ),
        out_shape=[
            jax.ShapeDtypeStruct((coarse * halves, count, 2, frames, inputs), jnp.bfloat16)
            for count in chunks
        ],
        grid=(coarse,),
        in_specs=[
            pl.BlockSpec((2, 1, inputs, block), lambda c: (0, c, 0, 0)),
            pl.BlockSpec((2, 1, FINE, inputs), lambda c: (0, c, 0, 0)),
            pl.BlockSpec(table.shape, lambda c: (0, 0)),
        ]
        + [pl.BlockSpec(memory_space=pl.ANY)] * len(waits),
        out_specs=[
            pl.BlockSpec((halves, count, 2, frames, inputs), lambda c: (c, 0, 0, 0, 0))
            for count in chunks
        ],
        scratch_shapes=[pltpu.VMEM((2, FINE, 2 * GROUP, inputs), jnp.float32)],
        compiler_params=pltpu.CompilerParams(vmem_limit_bytes=VMEM),
        cost_estimate=pl.CostEstimate(
            flops=4 * table.size * inputs * frames // GROUP * coarse,
            bytes_accessed=16 * coarse * inputs * frames * FINE,
            transcendentals=0,
        ),
        name="filter_bank",
    )(voltages, gains, jnp.asarray(table), *waits)


def gate(released, waits):
    def nothing(*_):
        pass

    anywhere = pl.BlockSpec(memory_space=pl.ANY)
    return pl.pallas_call(
        nothing,
        out_shape=[jax.ShapeDtypeStruct(array.shape, array.dtype) for array in released],
        in_specs=[anywhere] * (len(released) + len(waits)),
        out_specs=[anywhere] * len(released),
        input_output_aliases={index: index for index in range(len(released))},
        compiler_params=pltpu.CompilerParams(vmem_limit_bytes=VMEM),
        cost_estimate=pl.CostEstimate(flops=0, bytes_accessed=0, transcendentals=0),
        name="gate",
    )(*released, *waits)


def correlate_kernel(pieces, tile, scale, where_ref, *rest):
    blocks = rest[:pieces]
    out_ref, rows_ref = rest[-2:]
    inputs = blocks[0].shape[4]
    row_count, total = out_ref.shape[1:]
    depth = rows_ref.shape[1]
    per_tile = tile // inputs
    row_tiles, column_tiles = row_count // tile, total // tile

    def columns_of(position):
        sources = [position * per_tile + index for index in range(per_tile)]
        parts = [
            jnp.concatenate([block[source, 0, part] for source in sources], axis=1)
            for part in range(2)
            for block in blocks
        ]
        return jnp.concatenate(parts, axis=0)

    first_tile = where_ref[0] * row_tiles
    unit = (
        lax.broadcasted_iota(jnp.int32, (tile, tile), 0)
        == lax.broadcasted_iota(jnp.int32, (tile, tile), 1)
    )
    unit = jnp.where(unit, 1.0, 0.0).astype(jnp.bfloat16)
    for row in range(row_tiles):
        turned = columns_of(first_tile + row).T
        imag_at = slice(row * tile, (row + 1) * tile)
        real_at = slice(row_count + row * tile, row_count + (row + 1) * tile)
        rows_ref[real_at, :] = turned
        rows_ref[imag_at, : depth // 2] = turned[:, depth // 2 :]
        rows_ref[imag_at, depth // 2 :] = -turned[:, : depth // 2]

    def product(start, size, column):
        left = rows_ref[pl.ds(pl.multiple_of(start, tile), size), :]
        return jnp.dot(left, columns_of(column), preferred_element_type=jnp.float32) * scale

    before = first_tile > 0
    start = jnp.where(before, 0, row_count)
    first_column = jnp.where(before, 0, row_tiles)
    width = total - row_count
    right = jnp.concatenate([columns_of(first_column + index) for index in range(width // tile)], axis=1)
    column_at = pl.ds(pl.multiple_of(first_column * tile, tile), width)
    left = rows_ref[pl.ds(pl.multiple_of(start, tile), row_count), :]
    sums = jnp.dot(left, right, preferred_element_type=jnp.float32) * scale
    out_ref[0, :, column_at] = sums.astype(out_ref.dtype)
    upper = lax.broadcasted_iota(jnp.int32, (tile, tile), 0) <= lax.broadcasted_iota(jnp.int32, (tile, tile), 1)
    column_at = pl.ds(pl.multiple_of(first_tile * tile, tile), tile)
    sums = product(0, 3 * tile, first_tile)
    out_ref[0, :tile, column_at] = jnp.where(upper, sums[2 * tile :], sums[:tile]).astype(out_ref.dtype)
    out_ref[0, tile:, column_at] = sums[tile : 2 * tile].astype(out_ref.dtype)
    column_at = pl.ds(pl.multiple_of((first_tile + 1) * tile, tile), tile)
    sums = product(tile, 3 * tile, first_tile + 1)
    out_ref[0, :tile, column_at] = sums[tile : 2 * tile].astype(out_ref.dtype)
    out_ref[0, tile:, column_at] = jnp.where(upper, sums[2 * tile :], sums[:tile]).astype(out_ref.dtype)


def correlate(pieces, where, held, first, count, channels, row_count, total, tile, scale):
    sources, _, _, _, inputs = pieces[0][0].shape
    depth = 2 * sum(array.shape[3] for array, _ in pieces)
    operands = [array for array, _ in pieces]
    in_specs = [
        pl.BlockSpec((sources, 1, 2, array.shape[3], inputs), lambda q, w, start=start: (0, start + q, 0, 0, 0))
        for array, start in pieces
    ]
    aliases = {}
    if held is not None:
        aliases = {1 + len(operands): 0}
        operands.append(held)
        in_specs.append(pl.BlockSpec(memory_space=pl.ANY))
    return pl.pallas_call(
        functools.partial(correlate_kernel, len(pieces), tile, scale),
        out_shape=jax.ShapeDtypeStruct((channels, row_count, total), jnp.bfloat16),
        grid_spec=pltpu.PrefetchScalarGridSpec(
            num_scalar_prefetch=1,
            grid=(count,),
            in_specs=in_specs,
            out_specs=pl.BlockSpec((1, row_count, total), lambda q, w: (first + q, 0, 0)),
            scratch_shapes=[pltpu.VMEM((2 * row_count, depth), jnp.bfloat16)],
        ),
        input_output_aliases=aliases,
        compiler_params=pltpu.CompilerParams(vmem_limit_bytes=VMEM),
        cost_estimate=pl.CostEstimate(
            flops=count * 8 * row_count * total * depth,
            bytes_accessed=count * 16 * total * depth,
            transcendentals=0,
        ),
        name="correlate",
    )(where, *operands)


def chunk_sizes(channels):
    cuts = sorted({0} | {max(1, channels * part // 16) for part in PARTS})
    return [stop - start for start, stop in zip(cuts, cuts[1:])]


def local_kernels(count, spans, voltages, gains):
    coarse, inputs, samples = voltages.shape[1:]
    frames = samples // FINE
    halves = count // coarse
    channels = FINE // halves
    chunks = chunk_sizes(channels)
    total = count * inputs
    row_count = total // spans
    early = max(2 * GROUP, frames * EARLY // 16 // (2 * GROUP) * (2 * GROUP))
    scale = 1.0 / (spans * frames)
    where = jnp.stack([lax.axis_index("span")]).astype(jnp.int32)
    gains = jnp.swapaxes(gains, 2, 3)

    def across(array):
        return lax.all_to_all(array, "inp", split_axis=0, concat_axis=0, tiled=True)

    def other_spans(array):
        return [
            lax.ppermute(array, "span", [(i, i ^ other) for i in range(spans)]) for other in range(1, spans)
        ]

    outgoing = filter_bank(voltages, gains, halves, [channels], 0, early)
    outgoing = list(outgoing)
    outgoing += list(filter_bank(voltages, gains, halves, chunks, early, frames, outgoing))
    turned = across(outgoing[0])
    outgoing[1] = gate([outgoing[1]], [turned])[0]
    first_frames = [turned] + other_spans(turned)
    held, first = None, 0
    for index, size in enumerate(chunks):
        turned = across(outgoing[1 + index])
        if held is not None:
            turned, held = gate([turned, held], [])
        pieces = [(array, first) for array in first_frames]
        pieces += [(array, 0) for array in [turned] + other_spans(turned)]
        held = correlate(
            pieces, where, held, first, size, channels, row_count, total, 2 * LANES, scale
        )
        first += size
    return held


def power_of_two(number):
    return number > 0 and number & (number - 1) == 0


def solution(mesh):
    count, spans = mesh.shape["inp"], mesh.shape["span"]

    def local(voltages, gains):
        coarse, inputs, samples = voltages.shape[1:]
        fits = (
            power_of_two(count)
            and power_of_two(spans)
            and count % coarse == 0
            and power_of_two(count // coarse)
            and FINE % (count // coarse) == 0
            and (FINE // (count // coarse)) % 8 == 0
            and inputs == LANES
            and samples % (2 * GROUP * FINE) == 0
            and samples >= 8 * GROUP * FINE
            and count * inputs // spans == 4 * LANES
        )
        if fits:
            return local_kernels(count, spans, voltages, gains)
        return local_plain(voltages, gains)

    placed = (P(None, "beam", "inp", "span"), P(None, "beam", "inp", None))
    return jax.shard_map(
        local,
        mesh=mesh,
        in_specs=placed,
        out_specs=P(("beam", "inp"), "span", None),
        check_vma=False,
    )
```

```python
import functools
import math

import jax
import jax.numpy as jnp
import ml_dtypes
import numpy as np
from jax import lax
from jax.experimental import pallas as pl
from jax.experimental.pallas import tpu as pltpu
from jax.sharding import PartitionSpec as P

FINE = 32
TAPS = 4
LANES = 128
GROUP = 8
VMEM = 64 * 1024 * 1024 - 64 * 1024
UNROLL = 7
TOGETHER = 2
EARLY = 1
PARTS = (14, 16)


def prototype(tap_count, fine_count):
    length = tap_count * fine_count
    offsets = jnp.arange(length).astype(jnp.float32)
    shifted = (offsets - length / 2 + 0.5) / fine_count
    taper = 0.5 - 0.5 * jnp.cos(2.0 * math.pi * (offsets + 0.5) / length)
    window = jnp.sinc(shifted) * taper
    window = window / jnp.sqrt(jnp.sum(window * window))
    return window.reshape(tap_count, fine_count)


def kernels(window, fine_count):
    points = jnp.arange(fine_count)
    phase_steps = points[:, None] * points[None, :] % fine_count
    angles = 2.0 * math.pi * phase_steps.astype(jnp.float32) / fine_count
    cosine = jnp.cos(angles)
    sine_part = jnp.sin(angles)
    result = []
    for tap_index in range(window.shape[0]):
        weights = window[tap_index][:, None]
        hcos = weights * cosine
        hsin = weights * sine_part
        result.append(jnp.stack([jnp.stack([hcos, -hsin]), jnp.stack([hsin, hcos])]))
    return jnp.stack(result)


def packed_rows(left_rows, right_rows, left_all, row_start):
    real_sums = jnp.einsum("cif,cjf->cij", left_rows, left_all, preferred_element_type=jnp.float32)
    imag_sums = jnp.einsum("cif,cjf->cij", right_rows, left_all, preferred_element_type=jnp.float32)
    row_index = row_start + jnp.arange(left_rows.shape[1])
    col_index = jnp.arange(left_all.shape[1])
    upper = row_index[:, None] <= col_index[None, :]
    return jnp.where(upper[None], real_sums, imag_sums)


def local_plain(voltages, gains):
    coarse = voltages.shape[1]
    local_inputs = voltages.shape[2]
    samples = voltages.shape[3]
    frames = samples // FINE
    window = prototype(TAPS, FINE)
    filters = kernels(window, FINE)
    filter_table = jnp.transpose(filters, (1, 0, 3, 2, 4))
    filter_high = filter_table.astype(jnp.bfloat16)
    filter_low = (filter_table - filter_high.astype(jnp.float32)).astype(jnp.bfloat16)
    padded = jnp.pad(voltages, ((0, 0), (0, 0), (0, 0), (0, (TAPS - 1) * FINE)))
    stacked = jnp.stack(
        [padded[..., tap_index * FINE : tap_index * FINE + samples] for tap_index in range(TAPS)],
        axis=1,
    )
    stacked = stacked.reshape(2, TAPS, coarse, local_inputs, frames, FINE)
    spectra = jnp.einsum(
        "atcnmp,atpbk->bcknm", stacked, filter_high, preferred_element_type=jnp.float32
    )
    spectra = spectra + jnp.einsum(
        "atcnmp,atpbk->bcknm", stacked, filter_low, preferred_element_type=jnp.float32
    )
    gain_real = jnp.swapaxes(gains[0], 1, 2)[:, :, :, None]
    gain_imag = jnp.swapaxes(gains[1], 1, 2)[:, :, :, None]
    real_part = spectra[0] * gain_real - spectra[1] * gain_imag
    imag_part = spectra[0] * gain_imag + spectra[1] * gain_real
    outgoing = jnp.stack([real_part, imag_part]).astype(jnp.bfloat16)
    outgoing = outgoing.reshape(2, coarse * FINE, local_inputs, frames)
    turned = lax.all_to_all(outgoing, "inp", split_axis=1, concat_axis=2, tiled=True)
    inputs = turned.shape[2]
    span_count = lax.axis_size("span")
    row_count = inputs // span_count
    frame_scale = 1.0 / (span_count * frames)
    row_start = lax.axis_index("span") * row_count
    frame_piece = lax.all_gather(turned, "span", axis=3, tiled=True)
    left_all = jnp.concatenate([frame_piece[0], frame_piece[1]], axis=-1)
    own_rows = lax.dynamic_slice_in_dim(frame_piece, row_start, row_count, 2)
    left_rows = jnp.concatenate([own_rows[0], own_rows[1]], axis=-1)
    right_rows = jnp.concatenate([own_rows[1], -own_rows[0]], axis=-1)
    summed = packed_rows(left_rows, right_rows, left_all, row_start) * frame_scale
    return summed.astype(jnp.bfloat16)


def filter_rows():
    length = TAPS * FINE
    run = -(-(GROUP * FINE + length - FINE) // LANES) * LANES
    offsets = np.arange(length)
    window = np.sinc((offsets - length / 2 + 0.5) / FINE)
    window = window * (0.5 - 0.5 * np.cos(2.0 * np.pi * (offsets + 0.5) / length))
    window = window / np.sqrt(np.sum(window * window))
    angles = 2.0 * np.pi * (offsets[None, :] * np.arange(FINE)[:, None] % FINE) / FINE
    hcos = window * np.cos(angles)
    hsin = window * np.sin(angles)
    table = np.zeros((FINE, 2, GROUP, 2, run))
    for frame in range(GROUP):
        at = slice(frame * FINE, frame * FINE + length)
        table[:, 0, frame, 0, at] = hcos
        table[:, 0, frame, 1, at] = hsin
        table[:, 1, frame, 0, at] = -hsin
        table[:, 1, frame, 1, at] = hcos
    return table.reshape(-1, 2 * run).astype(ml_dtypes.bfloat16)


def filter_kernel(halves, chunks, lead, pairs, coarse, volt_ref, gain_ref, table_ref, *rest):
    outs, wide_ref = rest[-1 - len(chunks) : -1], rest[-1]
    inputs, samples = volt_ref.shape[2], volt_ref.shape[3]
    per_half = FINE // halves
    run = table_ref.shape[1] // 2
    hop = GROUP * FINE
    wide_ref[...] = jnp.broadcast_to(gain_ref[...][:, :, :, None, :], wide_ref.shape)

    def one(channel, pair, inside):
        sets = []
        for group in range(2):
            start = lead + (2 * pair + group) * hop
            columns = []
            for part in range(2):
                if inside:
                    columns.append(volt_ref[part, channel, :, pl.ds(pl.multiple_of(start, LANES), run)])
                else:
                    stop = min(start + run, samples)
                    columns.append(volt_ref[part, channel, :, start:stop])
                    if start + run > stop:
                        columns.append(jnp.zeros((inputs, start + run - stop), volt_ref.dtype))
            sets.append(jnp.concatenate(columns, axis=1))
        lines = jnp.concatenate(sets, axis=0)
        sums = lax.dot_general(
            table_ref[...], lines, (((1,), (1,)), ((), ())), preferred_element_type=jnp.float32
        )
        sums = sums.reshape(FINE, 2, GROUP, 2 * inputs)
        raw_real = jnp.concatenate([sums[:, 0, :, :inputs], sums[:, 0, :, inputs:]], axis=1)
        raw_imag = jnp.concatenate([sums[:, 1, :, :inputs], sums[:, 1, :, inputs:]], axis=1)
        gain_real, gain_imag = wide_ref[0, channel], wide_ref[1, channel]
        real = (raw_real * gain_real - raw_imag * gain_imag).astype(jnp.bfloat16)
        imag = (raw_real * gain_imag + raw_imag * gain_real).astype(jnp.bfloat16)
        frames = pl.ds(pl.multiple_of(2 * GROUP * pair, 2 * GROUP), 2 * GROUP) if inside else pl.ds(
            2 * GROUP * pair, 2 * GROUP
        )
        for half in range(halves):
            start = half * per_half
            for out, size in zip(outs, chunks):
                out[channel * halves + half, :, 0, frames, :] = real[start : start + size]
                out[channel * halves + half, :, 1, frames, :] = imag[start : start + size]
                start += size

    whole = min(pairs, (samples - lead - run + hop) // (2 * hop))

    for channel in range(coarse):

        def loop(pair, _, channel=channel):
            one(channel, pair, True)
            return 0

        lax.fori_loop(0, whole, loop, 0, unroll=UNROLL)
        for pair in range(whole, pairs):
            one(channel, pair, False)


def filter_bank(voltages, gains, halves, chunks, first_frame, last_frame, together, waits=()):
    _, coarse, inputs, samples = voltages.shape
    table = filter_rows()
    run = table.shape[1] // 2
    frames = last_frame - first_frame
    ahead = run - GROUP * FINE
    block = min(samples, last_frame * FINE + ahead)
    return pl.pallas_call(
        functools.partial(
            filter_kernel, halves, chunks, first_frame * FINE, frames // (2 * GROUP), together
        ),
        out_shape=[
            jax.ShapeDtypeStruct((coarse * halves, count, 2, frames, inputs), jnp.bfloat16)
            for count in chunks
        ],
        grid=(coarse // together,),
        in_specs=[
            pl.BlockSpec((2, together, inputs, block), lambda c: (0, c, 0, 0)),
            pl.BlockSpec((2, together, FINE, inputs), lambda c: (0, c, 0, 0)),
            pl.BlockSpec(table.shape, lambda c: (0, 0)),
        ]
        + [pl.BlockSpec(memory_space=pl.ANY)] * len(waits),
        out_specs=[
            pl.BlockSpec((together * halves, count, 2, frames, inputs), lambda c: (c, 0, 0, 0, 0))
            for count in chunks
        ],
        scratch_shapes=[pltpu.VMEM((2, together, FINE, 2 * GROUP, inputs), jnp.float32)],
        compiler_params=pltpu.CompilerParams(vmem_limit_bytes=VMEM),
        cost_estimate=pl.CostEstimate(
            flops=4 * table.size * inputs * frames // GROUP * coarse,
            bytes_accessed=16 * coarse * inputs * frames * FINE,
            transcendentals=0,
        ),
        name="filter_bank",
    )(voltages, gains, jnp.asarray(table), *waits)


def gate(released, waits):
    def nothing(*_):
        pass

    anywhere = pl.BlockSpec(memory_space=pl.ANY)
    return pl.pallas_call(
        nothing,
        out_shape=[jax.ShapeDtypeStruct(array.shape, array.dtype) for array in released],
        in_specs=[anywhere] * (len(released) + len(waits)),
        out_specs=[anywhere] * len(released),
        input_output_aliases={index: index for index in range(len(released))},
        compiler_params=pltpu.CompilerParams(vmem_limit_bytes=VMEM),
        cost_estimate=pl.CostEstimate(flops=0, bytes_accessed=0, transcendentals=0),
        name="gate",
    )(*released, *waits)


def correlate_kernel(pieces, tile, scale, where_ref, *rest):
    blocks = rest[:pieces]
    out_ref, rows_ref = rest[-2:]
    inputs = blocks[0].shape[4]
    row_count, total = out_ref.shape[1:]
    depth = rows_ref.shape[1]
    per_tile = tile // inputs
    row_tiles, column_tiles = row_count // tile, total // tile

    def columns_of(position):
        sources = [position * per_tile + index for index in range(per_tile)]
        parts = [
            jnp.concatenate([block[source, 0, part] for source in sources], axis=1)
            for part in range(2)
            for block in blocks
        ]
        return jnp.concatenate(parts, axis=0)

    first_tile = where_ref[0] * row_tiles
    unit = (
        lax.broadcasted_iota(jnp.int32, (tile, tile), 0)
        == lax.broadcasted_iota(jnp.int32, (tile, tile), 1)
    )
    unit = jnp.where(unit, 1.0, 0.0).astype(jnp.bfloat16)
    for row in range(row_tiles):
        turned = columns_of(first_tile + row).T
        imag_at = slice(row * tile, (row + 1) * tile)
        real_at = slice(row_count + row * tile, row_count + (row + 1) * tile)
        rows_ref[real_at, :] = turned
        rows_ref[imag_at, : depth // 2] = turned[:, depth // 2 :]
        rows_ref[imag_at, depth // 2 :] = -turned[:, : depth // 2]

    def product(start, size, column):
        left = rows_ref[pl.ds(pl.multiple_of(start, tile), size), :]
        return jnp.dot(left, columns_of(column), preferred_element_type=jnp.float32) * scale

    before = first_tile > 0
    start = jnp.where(before, 0, row_count)
    first_column = jnp.where(before, 0, row_tiles)
    width = total - row_count
    right = jnp.concatenate([columns_of(first_column + index) for index in range(width // tile)], axis=1)
    column_at = pl.ds(pl.multiple_of(first_column * tile, tile), width)
    left = rows_ref[pl.ds(pl.multiple_of(start, tile), row_count), :]
    sums = jnp.dot(left, right, preferred_element_type=jnp.float32) * scale
    out_ref[0, :, column_at] = sums.astype(out_ref.dtype)
    upper = lax.broadcasted_iota(jnp.int32, (tile, tile), 0) <= lax.broadcasted_iota(jnp.int32, (tile, tile), 1)
    column_at = pl.ds(pl.multiple_of(first_tile * tile, tile), tile)
    sums = product(0, 3 * tile, first_tile)
    out_ref[0, :tile, column_at] = jnp.where(upper, sums[2 * tile :], sums[:tile]).astype(out_ref.dtype)
    out_ref[0, tile:, column_at] = sums[tile : 2 * tile].astype(out_ref.dtype)
    column_at = pl.ds(pl.multiple_of((first_tile + 1) * tile, tile), tile)
    sums = product(tile, 3 * tile, first_tile + 1)
    out_ref[0, :tile, column_at] = sums[tile : 2 * tile].astype(out_ref.dtype)
    out_ref[0, tile:, column_at] = jnp.where(upper, sums[2 * tile :], sums[:tile]).astype(out_ref.dtype)


def correlate(pieces, where, held, first, count, channels, row_count, total, tile, scale):
    sources, _, _, _, inputs = pieces[0][0].shape
    depth = 2 * sum(array.shape[3] for array, _ in pieces)
    operands = [array for array, _ in pieces]
    in_specs = [
        pl.BlockSpec((sources, 1, 2, array.shape[3], inputs), lambda q, w, start=start: (0, start + q, 0, 0, 0))
        for array, start in pieces
    ]
    aliases = {}
    if held is not None:
        aliases = {1 + len(operands): 0}
        operands.append(held)
        in_specs.append(pl.BlockSpec(memory_space=pl.ANY))
    return pl.pallas_call(
        functools.partial(correlate_kernel, len(pieces), tile, scale),
        out_shape=jax.ShapeDtypeStruct((channels, row_count, total), jnp.bfloat16),
        grid_spec=pltpu.PrefetchScalarGridSpec(
            num_scalar_prefetch=1,
            grid=(count,),
            in_specs=in_specs,
            out_specs=pl.BlockSpec((1, row_count, total), lambda q, w: (first + q, 0, 0)),
            scratch_shapes=[pltpu.VMEM((2 * row_count, depth), jnp.bfloat16)],
        ),
        input_output_aliases=aliases,
        compiler_params=pltpu.CompilerParams(vmem_limit_bytes=VMEM),
        cost_estimate=pl.CostEstimate(
            flops=count * 8 * row_count * total * depth,
            bytes_accessed=count * 16 * total * depth,
            transcendentals=0,
        ),
        name="correlate",
    )(where, *operands)


def chunk_sizes(channels):
    cuts = sorted({0} | {max(1, channels * part // 16) for part in PARTS})
    return [stop - start for start, stop in zip(cuts, cuts[1:])]


def local_kernels(count, spans, voltages, gains):
    coarse, inputs, samples = voltages.shape[1:]
    frames = samples // FINE
    halves = count // coarse
    channels = FINE // halves
    chunks = chunk_sizes(channels)
    total = count * inputs
    row_count = total // spans
    early = max(2 * GROUP, frames * EARLY // 16 // (2 * GROUP) * (2 * GROUP))
    scale = 1.0 / (spans * frames)
    where = jnp.stack([lax.axis_index("span")]).astype(jnp.int32)
    gains = jnp.swapaxes(gains, 2, 3)

    def across(array):
        return lax.all_to_all(array, "inp", split_axis=0, concat_axis=0, tiled=True)

    def other_spans(array):
        return [
            lax.ppermute(array, "span", [(i, i ^ other) for i in range(spans)]) for other in range(1, spans)
        ]

    outgoing = filter_bank(voltages, gains, halves, [channels], 0, early, TOGETHER if coarse % TOGETHER == 0 else 1)
    outgoing = list(outgoing)
    outgoing += list(filter_bank(voltages, gains, halves, chunks, early, frames, 1, outgoing))
    turned = across(outgoing[0])
    outgoing[1] = gate([outgoing[1]], [turned])[0]
    first_frames = [turned] + other_spans(turned)
    held, first = None, 0
    for index, size in enumerate(chunks):
        turned = across(outgoing[1 + index])
        if held is not None:
            turned, held = gate([turned, held], [])
        pieces = [(array, first) for array in first_frames]
        pieces += [(array, 0) for array in [turned] + other_spans(turned)]
        held = correlate(
            pieces, where, held, first, size, channels, row_count, total, 2 * LANES, scale
        )
        first += size
    return held


def power_of_two(number):
    return number > 0 and number & (number - 1) == 0


def solution(mesh):
    count, spans = mesh.shape["inp"], mesh.shape["span"]

    def local(voltages, gains):
        coarse, inputs, samples = voltages.shape[1:]
        fits = (
            power_of_two(count)
            and power_of_two(spans)
            and count % coarse == 0
            and power_of_two(count // coarse)
            and FINE % (count // coarse) == 0
            and (FINE // (count // coarse)) % 8 == 0
            and inputs == LANES
            and samples % (2 * GROUP * FINE) == 0
            and samples >= 8 * GROUP * FINE
            and count * inputs // spans == 4 * LANES
        )
        if fits:
            return local_kernels(count, spans, voltages, gains)
        return local_plain(voltages, gains)

    placed = (P(None, "beam", "inp", "span"), P(None, "beam", "inp", None))
    return jax.shard_map(
        local,
        mesh=mesh,
        in_specs=placed,
        out_specs=P(("beam", "inp"), "span", None),
        check_vma=False,
    )
```

```python
import functools
import math

import jax
import jax.numpy as jnp
import ml_dtypes
import numpy as np
from jax import lax
from jax.experimental import pallas as pl
from jax.experimental.pallas import tpu as pltpu
from jax.sharding import PartitionSpec as P

FINE = 32
TAPS = 4
LANES = 128
GROUP = 8
VMEM = 64 * 1024 * 1024 - 64 * 1024
UNROLL = 7
TOGETHER = 2
EARLY = 1
PARTS = (14, 16)


def prototype(tap_count, fine_count):
    length = tap_count * fine_count
    offsets = jnp.arange(length).astype(jnp.float32)
    shifted = (offsets - length / 2 + 0.5) / fine_count
    taper = 0.5 - 0.5 * jnp.cos(2.0 * math.pi * (offsets + 0.5) / length)
    window = jnp.sinc(shifted) * taper
    window = window / jnp.sqrt(jnp.sum(window * window))
    return window.reshape(tap_count, fine_count)


def kernels(window, fine_count):
    points = jnp.arange(fine_count)
    phase_steps = points[:, None] * points[None, :] % fine_count
    angles = 2.0 * math.pi * phase_steps.astype(jnp.float32) / fine_count
    cosine = jnp.cos(angles)
    sine_part = jnp.sin(angles)
    result = []
    for tap_index in range(window.shape[0]):
        weights = window[tap_index][:, None]
        hcos = weights * cosine
        hsin = weights * sine_part
        result.append(jnp.stack([jnp.stack([hcos, -hsin]), jnp.stack([hsin, hcos])]))
    return jnp.stack(result)


def packed_rows(left_rows, right_rows, left_all, row_start):
    real_sums = jnp.einsum("cif,cjf->cij", left_rows, left_all, preferred_element_type=jnp.float32)
    imag_sums = jnp.einsum("cif,cjf->cij", right_rows, left_all, preferred_element_type=jnp.float32)
    row_index = row_start + jnp.arange(left_rows.shape[1])
    col_index = jnp.arange(left_all.shape[1])
    upper = row_index[:, None] <= col_index[None, :]
    return jnp.where(upper[None], real_sums, imag_sums)


def local_plain(voltages, gains):
    coarse = voltages.shape[1]
    local_inputs = voltages.shape[2]
    samples = voltages.shape[3]
    frames = samples // FINE
    window = prototype(TAPS, FINE)
    filters = kernels(window, FINE)
    filter_table = jnp.transpose(filters, (1, 0, 3, 2, 4))
    filter_high = filter_table.astype(jnp.bfloat16)
    filter_low = (filter_table - filter_high.astype(jnp.float32)).astype(jnp.bfloat16)
    padded = jnp.pad(voltages, ((0, 0), (0, 0), (0, 0), (0, (TAPS - 1) * FINE)))
    stacked = jnp.stack(
        [padded[..., tap_index * FINE : tap_index * FINE + samples] for tap_index in range(TAPS)],
        axis=1,
    )
    stacked = stacked.reshape(2, TAPS, coarse, local_inputs, frames, FINE)
    spectra = jnp.einsum(
        "atcnmp,atpbk->bcknm", stacked, filter_high, preferred_element_type=jnp.float32
    )
    spectra = spectra + jnp.einsum(
        "atcnmp,atpbk->bcknm", stacked, filter_low, preferred_element_type=jnp.float32
    )
    gain_real = jnp.swapaxes(gains[0], 1, 2)[:, :, :, None]
    gain_imag = jnp.swapaxes(gains[1], 1, 2)[:, :, :, None]
    real_part = spectra[0] * gain_real - spectra[1] * gain_imag
    imag_part = spectra[0] * gain_imag + spectra[1] * gain_real
    outgoing = jnp.stack([real_part, imag_part]).astype(jnp.bfloat16)
    outgoing = outgoing.reshape(2, coarse * FINE, local_inputs, frames)
    turned = lax.all_to_all(outgoing, "inp", split_axis=1, concat_axis=2, tiled=True)
    inputs = turned.shape[2]
    span_count = lax.axis_size("span")
    row_count = inputs // span_count
    frame_scale = 1.0 / (span_count * frames)
    row_start = lax.axis_index("span") * row_count
    frame_piece = lax.all_gather(turned, "span", axis=3, tiled=True)
    left_all = jnp.concatenate([frame_piece[0], frame_piece[1]], axis=-1)
    own_rows = lax.dynamic_slice_in_dim(frame_piece, row_start, row_count, 2)
    left_rows = jnp.concatenate([own_rows[0], own_rows[1]], axis=-1)
    right_rows = jnp.concatenate([own_rows[1], -own_rows[0]], axis=-1)
    summed = packed_rows(left_rows, right_rows, left_all, row_start) * frame_scale
    return summed.astype(jnp.bfloat16)


def filter_rows():
    length = TAPS * FINE
    run = -(-(GROUP * FINE + length - FINE) // LANES) * LANES
    offsets = np.arange(length)
    window = np.sinc((offsets - length / 2 + 0.5) / FINE)
    window = window * (0.5 - 0.5 * np.cos(2.0 * np.pi * (offsets + 0.5) / length))
    window = window / np.sqrt(np.sum(window * window))
    angles = 2.0 * np.pi * (offsets[None, :] * np.arange(FINE)[:, None] % FINE) / FINE
    hcos = window * np.cos(angles)
    hsin = window * np.sin(angles)
    table = np.zeros((FINE, 2, GROUP, 2, run))
    for frame in range(GROUP):
        at = slice(frame * FINE, frame * FINE + length)
        table[:, 0, frame, 0, at] = hcos
        table[:, 0, frame, 1, at] = hsin
        table[:, 1, frame, 0, at] = -hsin
        table[:, 1, frame, 1, at] = hcos
    return table.reshape(-1, 2 * run).astype(ml_dtypes.bfloat16)


def filter_kernel(halves, chunks, firsts, pairs, coarse, volt_ref, gain_ref, table_ref, *rest):
    outs, wide_ref = rest[-1 - len(chunks) : -1], rest[-1]
    inputs, samples = volt_ref.shape[2], volt_ref.shape[3]
    per_half = FINE // halves
    run = table_ref.shape[1] // 2
    hop = GROUP * FINE
    wide_ref[...] = jnp.broadcast_to(gain_ref[...][:, :, :, None, :], wide_ref.shape)

    def one(channel, pair, inside):
        sets = []
        for group in range(2):
            start = (2 * pair + group) * hop
            columns = []
            for part in range(2):
                if inside:
                    columns.append(volt_ref[part, channel, :, pl.ds(pl.multiple_of(start, LANES), run)])
                else:
                    stop = min(start + run, samples)
                    columns.append(volt_ref[part, channel, :, start:stop])
                    if start + run > stop:
                        columns.append(jnp.zeros((inputs, start + run - stop), volt_ref.dtype))
            sets.append(jnp.concatenate(columns, axis=1))
        lines = jnp.concatenate(sets, axis=0)
        sums = lax.dot_general(
            table_ref[...], lines, (((1,), (1,)), ((), ())), preferred_element_type=jnp.float32
        )
        sums = sums.reshape(FINE, 2, GROUP, 2 * inputs)
        raw_real = jnp.concatenate([sums[:, 0, :, :inputs], sums[:, 0, :, inputs:]], axis=1)
        raw_imag = jnp.concatenate([sums[:, 1, :, :inputs], sums[:, 1, :, inputs:]], axis=1)
        gain_real, gain_imag = wide_ref[0, channel], wide_ref[1, channel]
        real = (raw_real * gain_real - raw_imag * gain_imag).astype(jnp.bfloat16)
        imag = (raw_real * gain_imag + raw_imag * gain_real).astype(jnp.bfloat16)
        for half in range(halves):
            start = half * per_half
            for out, size, first in zip(outs, chunks, firsts):
                if not inside and pair < first:
                    start += size
                    continue
                at = 2 * GROUP * (pair - first)
                frames = pl.ds(pl.multiple_of(at, 2 * GROUP) if inside else at, 2 * GROUP)
                out[channel * halves + half, :, 0, frames, :] = real[start : start + size]
                out[channel * halves + half, :, 1, frames, :] = imag[start : start + size]
                start += size

    whole = min(pairs, (samples - run + hop) // (2 * hop))
    common = max(firsts)

    for channel in range(coarse):

        def loop(pair, _, channel=channel):
            one(channel, pair, True)
            return 0

        for pair in range(min(firsts), common):
            one(channel, pair, False)
        lax.fori_loop(common, whole, loop, 0, unroll=UNROLL)
        for pair in range(whole, pairs):
            one(channel, pair, False)


def filter_bank(voltages, gains, halves, chunks, first_frames, last_frame, together, waits=()):
    _, coarse, inputs, samples = voltages.shape
    table = filter_rows()
    run = table.shape[1] // 2
    ahead = run - GROUP * FINE
    block = min(samples, last_frame * FINE + ahead)
    return pl.pallas_call(
        functools.partial(
            filter_kernel,
            halves,
            chunks,
            [first // (2 * GROUP) for first in first_frames],
            last_frame // (2 * GROUP),
            together,
        ),
        out_shape=[
            jax.ShapeDtypeStruct((coarse * halves, count, 2, last_frame - first, inputs), jnp.bfloat16)
            for count, first in zip(chunks, first_frames)
        ],
        grid=(coarse // together,),
        in_specs=[
            pl.BlockSpec((2, together, inputs, block), lambda c: (0, c, 0, 0)),
            pl.BlockSpec((2, together, FINE, inputs), lambda c: (0, c, 0, 0)),
            pl.BlockSpec(table.shape, lambda c: (0, 0)),
        ]
        + [pl.BlockSpec(memory_space=pl.ANY)] * len(waits),
        out_specs=[
            pl.BlockSpec((together * halves, count, 2, last_frame - first, inputs), lambda c: (c, 0, 0, 0, 0))
            for count, first in zip(chunks, first_frames)
        ],
        scratch_shapes=[pltpu.VMEM((2, together, FINE, 2 * GROUP, inputs), jnp.float32)],
        compiler_params=pltpu.CompilerParams(vmem_limit_bytes=VMEM),
        cost_estimate=pl.CostEstimate(
            flops=4 * table.size * inputs * last_frame // GROUP * coarse,
            bytes_accessed=16 * coarse * inputs * last_frame * FINE,
            transcendentals=0,
        ),
        name="filter_bank",
    )(voltages, gains, jnp.asarray(table), *waits)


def gate(released, waits):
    def nothing(*_):
        pass

    anywhere = pl.BlockSpec(memory_space=pl.ANY)
    return pl.pallas_call(
        nothing,
        out_shape=[jax.ShapeDtypeStruct(array.shape, array.dtype) for array in released],
        in_specs=[anywhere] * (len(released) + len(waits)),
        out_specs=[anywhere] * len(released),
        input_output_aliases={index: index for index in range(len(released))},
        compiler_params=pltpu.CompilerParams(vmem_limit_bytes=VMEM),
        cost_estimate=pl.CostEstimate(flops=0, bytes_accessed=0, transcendentals=0),
        name="gate",
    )(*released, *waits)


def correlate_kernel(pieces, tile, scale, added, where_ref, *rest):
    blocks = rest[:pieces]
    added_ref = rest[pieces] if added else None
    out_ref, rows_ref = rest[-2:]
    inputs = blocks[0].shape[4]
    row_count, total = out_ref.shape[1:]
    depth = rows_ref.shape[1]
    per_tile = tile // inputs
    row_tiles, column_tiles = row_count // tile, total // tile

    def columns_of(position):
        sources = [position * per_tile + index for index in range(per_tile)]
        parts = [
            jnp.concatenate([block[source, 0, part] for source in sources], axis=1)
            for part in range(2)
            for block in blocks
        ]
        return jnp.concatenate(parts, axis=0)

    first_tile = where_ref[0] * row_tiles
    unit = (
        lax.broadcasted_iota(jnp.int32, (tile, tile), 0)
        == lax.broadcasted_iota(jnp.int32, (tile, tile), 1)
    )
    unit = jnp.where(unit, 1.0, 0.0).astype(jnp.bfloat16)
    for row in range(row_tiles):
        turned = columns_of(first_tile + row).T
        imag_at = slice(row * tile, (row + 1) * tile)
        real_at = slice(row_count + row * tile, row_count + (row + 1) * tile)
        rows_ref[real_at, :] = turned
        rows_ref[imag_at, : depth // 2] = turned[:, depth // 2 :]
        rows_ref[imag_at, depth // 2 :] = -turned[:, : depth // 2]

    def product(start, size, column):
        left = rows_ref[pl.ds(pl.multiple_of(start, tile), size), :]
        return jnp.dot(left, columns_of(column), preferred_element_type=jnp.float32)

    def store(at, column_at, sums):
        if added:
            sums = sums + added_ref[0, at, column_at]
        out_ref[0, at, column_at] = (sums * scale if scale != 1.0 else sums).astype(out_ref.dtype)

    before = first_tile > 0
    start = jnp.where(before, 0, row_count)
    first_column = jnp.where(before, 0, row_tiles)
    width = total - row_count
    right = jnp.concatenate([columns_of(first_column + index) for index in range(width // tile)], axis=1)
    column_at = pl.ds(pl.multiple_of(first_column * tile, tile), width)
    left = rows_ref[pl.ds(pl.multiple_of(start, tile), row_count), :]
    store(slice(0, row_count), column_at, jnp.dot(left, right, preferred_element_type=jnp.float32))
    upper = lax.broadcasted_iota(jnp.int32, (tile, tile), 0) <= lax.broadcasted_iota(jnp.int32, (tile, tile), 1)
    column_at = pl.ds(pl.multiple_of(first_tile * tile, tile), tile)
    sums = product(0, 3 * tile, first_tile)
    store(slice(0, tile), column_at, jnp.where(upper, sums[2 * tile :], sums[:tile]))
    store(slice(tile, row_count), column_at, sums[tile : 2 * tile])
    column_at = pl.ds(pl.multiple_of((first_tile + 1) * tile, tile), tile)
    sums = product(tile, 3 * tile, first_tile + 1)
    store(slice(0, tile), column_at, sums[tile : 2 * tile])
    store(slice(tile, row_count), column_at, jnp.where(upper, sums[2 * tile :], sums[:tile]))


def correlate(pieces, where, held, first, count, channels, row_count, total, tile, scale, added=None, dtype=jnp.bfloat16):
    sources, _, _, _, inputs = pieces[0][0].shape
    depth = 2 * sum(array.shape[3] for array, _ in pieces)
    operands = [array for array, _ in pieces]
    in_specs = [
        pl.BlockSpec((sources, 1, 2, array.shape[3], inputs), lambda q, w, start=start: (0, start + q, 0, 0, 0))
        for array, start in pieces
    ]
    if added is not None:
        operands.append(added)
        in_specs.append(pl.BlockSpec((1, row_count, total), lambda q, w: (q, 0, 0)))
    aliases = {}
    if held is not None:
        aliases = {1 + len(operands): 0}
        operands.append(held)
        in_specs.append(pl.BlockSpec(memory_space=pl.ANY))
    return pl.pallas_call(
        functools.partial(correlate_kernel, len(pieces), tile, scale, added is not None),
        out_shape=jax.ShapeDtypeStruct((channels, row_count, total), dtype),
        grid_spec=pltpu.PrefetchScalarGridSpec(
            num_scalar_prefetch=1,
            grid=(count,),
            in_specs=in_specs,
            out_specs=pl.BlockSpec((1, row_count, total), lambda q, w: (first + q, 0, 0)),
            scratch_shapes=[pltpu.VMEM((2 * row_count, depth), jnp.bfloat16)],
        ),
        input_output_aliases=aliases,
        compiler_params=pltpu.CompilerParams(vmem_limit_bytes=VMEM),
        cost_estimate=pl.CostEstimate(
            flops=count * 8 * row_count * total * depth,
            bytes_accessed=count * 16 * total * depth,
            transcendentals=0,
        ),
        name="correlate",
    )(where, *operands)


def chunk_sizes(channels):
    cuts = sorted({0} | {max(1, channels * part // 16) for part in PARTS})
    return [stop - start for start, stop in zip(cuts, cuts[1:])]


def local_kernels(count, spans, voltages, gains):
    coarse, inputs, samples = voltages.shape[1:]
    frames = samples // FINE
    halves = count // coarse
    channels = FINE // halves
    chunks = chunk_sizes(channels)
    total = count * inputs
    row_count = total // spans
    early = max(2 * GROUP, frames * EARLY // 16 // (2 * GROUP) * (2 * GROUP))
    scale = 1.0 / (spans * frames)
    where = jnp.stack([lax.axis_index("span")]).astype(jnp.int32)
    gains = jnp.swapaxes(gains, 2, 3)

    def across(array):
        return lax.all_to_all(array, "inp", split_axis=0, concat_axis=0, tiled=True)

    def other_spans(array):
        return [
            lax.ppermute(array, "span", [(i, i ^ other) for i in range(spans)]) for other in range(1, spans)
        ]

    ahead = chunks[:-1] if len(chunks) > 1 else chunks
    begins = [early] * len(ahead) + [0] * (len(chunks) - len(ahead))
    outgoing = filter_bank(voltages, gains, halves, [sum(ahead)], [0], early, TOGETHER if coarse % TOGETHER == 0 else 1)
    outgoing = list(outgoing)
    outgoing += list(filter_bank(voltages, gains, halves, chunks, begins, frames, 1, outgoing))
    turned = across(outgoing[0])
    outgoing[1] = gate([outgoing[1]], [turned])[0]
    first_frames = [turned] + other_spans(turned)
    held, first = None, 0
    for index, size in enumerate(chunks):
        turned = across(outgoing[1 + index])
        if held is not None:
            turned, held = gate([turned, held], [])
        others = other_spans(turned)
        pieces = [(array, first) for array in first_frames] if begins[index] else []
        added = None
        if pieces:
            pieces += [(turned, 0)] + [(array, 0) for array in others]
        else:
            added = correlate(
                [(turned, 0)], where, None, 0, size, size, row_count, total, 2 * LANES, 1.0, None, jnp.float32
            )
            pieces = [(array, 0) for array in others]
        held = correlate(
            pieces, where, held, first, size, channels, row_count, total, 2 * LANES, scale, added
        )
        first += size
    return held


def power_of_two(number):
    return number > 0 and number & (number - 1) == 0


def solution(mesh):
    count, spans = mesh.shape["inp"], mesh.shape["span"]

    def local(voltages, gains):
        coarse, inputs, samples = voltages.shape[1:]
        fits = (
            power_of_two(count)
            and power_of_two(spans)
            and count % coarse == 0
            and power_of_two(count // coarse)
            and FINE % (count // coarse) == 0
            and (FINE // (count // coarse)) % 8 == 0
            and inputs == LANES
            and spans > 1
            and samples % (2 * GROUP * FINE) == 0
            and samples >= 8 * GROUP * FINE
            and count * inputs // spans == 4 * LANES
        )
        if fits:
            return local_kernels(count, spans, voltages, gains)
        return local_plain(voltages, gains)

    placed = (P(None, "beam", "inp", "span"), P(None, "beam", "inp", None))
    return jax.shard_map(
        local,
        mesh=mesh,
        in_specs=placed,
        out_specs=P(("beam", "inp"), "span", None),
        check_vma=False,
    )
```

```python
import functools
import math

import jax
import jax.numpy as jnp
import ml_dtypes
import numpy as np
from jax import lax
from jax.experimental import pallas as pl
from jax.experimental.pallas import tpu as pltpu
from jax.sharding import PartitionSpec as P

FINE = 32
TAPS = 4
LANES = 128
GROUP = 8
VMEM = 64 * 1024 * 1024 - 64 * 1024
UNROLL = 7
TOGETHER = 2
EARLY = 1
PARTS = (14, 16)


def prototype(tap_count, fine_count):
    length = tap_count * fine_count
    offsets = jnp.arange(length).astype(jnp.float32)
    shifted = (offsets - length / 2 + 0.5) / fine_count
    taper = 0.5 - 0.5 * jnp.cos(2.0 * math.pi * (offsets + 0.5) / length)
    window = jnp.sinc(shifted) * taper
    window = window / jnp.sqrt(jnp.sum(window * window))
    return window.reshape(tap_count, fine_count)


def kernels(window, fine_count):
    points = jnp.arange(fine_count)
    phase_steps = points[:, None] * points[None, :] % fine_count
    angles = 2.0 * math.pi * phase_steps.astype(jnp.float32) / fine_count
    cosine = jnp.cos(angles)
    sine_part = jnp.sin(angles)
    result = []
    for tap_index in range(window.shape[0]):
        weights = window[tap_index][:, None]
        hcos = weights * cosine
        hsin = weights * sine_part
        result.append(jnp.stack([jnp.stack([hcos, -hsin]), jnp.stack([hsin, hcos])]))
    return jnp.stack(result)


def packed_rows(left_rows, right_rows, left_all, row_start):
    real_sums = jnp.einsum("cif,cjf->cij", left_rows, left_all, preferred_element_type=jnp.float32)
    imag_sums = jnp.einsum("cif,cjf->cij", right_rows, left_all, preferred_element_type=jnp.float32)
    row_index = row_start + jnp.arange(left_rows.shape[1])
    col_index = jnp.arange(left_all.shape[1])
    upper = row_index[:, None] <= col_index[None, :]
    return jnp.where(upper[None], real_sums, imag_sums)


def local_plain(voltages, gains):
    coarse = voltages.shape[1]
    local_inputs = voltages.shape[2]
    samples = voltages.shape[3]
    frames = samples // FINE
    window = prototype(TAPS, FINE)
    filters = kernels(window, FINE)
    filter_table = jnp.transpose(filters, (1, 0, 3, 2, 4))
    filter_high = filter_table.astype(jnp.bfloat16)
    filter_low = (filter_table - filter_high.astype(jnp.float32)).astype(jnp.bfloat16)
    padded = jnp.pad(voltages, ((0, 0), (0, 0), (0, 0), (0, (TAPS - 1) * FINE)))
    stacked = jnp.stack(
        [padded[..., tap_index * FINE : tap_index * FINE + samples] for tap_index in range(TAPS)],
        axis=1,
    )
    stacked = stacked.reshape(2, TAPS, coarse, local_inputs, frames, FINE)
    spectra = jnp.einsum(
        "atcnmp,atpbk->bcknm", stacked, filter_high, preferred_element_type=jnp.float32
    )
    spectra = spectra + jnp.einsum(
        "atcnmp,atpbk->bcknm", stacked, filter_low, preferred_element_type=jnp.float32
    )
    gain_real = jnp.swapaxes(gains[0], 1, 2)[:, :, :, None]
    gain_imag = jnp.swapaxes(gains[1], 1, 2)[:, :, :, None]
    real_part = spectra[0] * gain_real - spectra[1] * gain_imag
    imag_part = spectra[0] * gain_imag + spectra[1] * gain_real
    outgoing = jnp.stack([real_part, imag_part]).astype(jnp.bfloat16)
    outgoing = outgoing.reshape(2, coarse * FINE, local_inputs, frames)
    turned = lax.all_to_all(outgoing, "inp", split_axis=1, concat_axis=2, tiled=True)
    inputs = turned.shape[2]
    span_count = lax.axis_size("span")
    row_count = inputs // span_count
    frame_scale = 1.0 / (span_count * frames)
    row_start = lax.axis_index("span") * row_count
    frame_piece = lax.all_gather(turned, "span", axis=3, tiled=True)
    left_all = jnp.concatenate([frame_piece[0], frame_piece[1]], axis=-1)
    own_rows = lax.dynamic_slice_in_dim(frame_piece, row_start, row_count, 2)
    left_rows = jnp.concatenate([own_rows[0], own_rows[1]], axis=-1)
    right_rows = jnp.concatenate([own_rows[1], -own_rows[0]], axis=-1)
    summed = packed_rows(left_rows, right_rows, left_all, row_start) * frame_scale
    return summed.astype(jnp.bfloat16)


def filter_rows():
    length = TAPS * FINE
    run = -(-(GROUP * FINE + length - FINE) // LANES) * LANES
    offsets = np.arange(length)
    window = np.sinc((offsets - length / 2 + 0.5) / FINE)
    window = window * (0.5 - 0.5 * np.cos(2.0 * np.pi * (offsets + 0.5) / length))
    window = window / np.sqrt(np.sum(window * window))
    angles = 2.0 * np.pi * (offsets[None, :] * np.arange(FINE)[:, None] % FINE) / FINE
    hcos = window * np.cos(angles)
    hsin = window * np.sin(angles)
    table = np.zeros((FINE, 2, GROUP, 2, run))
    for frame in range(GROUP):
        at = slice(frame * FINE, frame * FINE + length)
        table[:, 0, frame, 0, at] = hcos
        table[:, 0, frame, 1, at] = hsin
        table[:, 1, frame, 0, at] = -hsin
        table[:, 1, frame, 1, at] = hcos
    return table.reshape(-1, 2 * run).astype(ml_dtypes.bfloat16)


def filter_kernel(halves, chunks, firsts, pairs, coarse, volt_ref, gain_ref, table_ref, *rest):
    outs, wide_ref = rest[-1 - len(chunks) : -1], rest[-1]
    inputs, samples = volt_ref.shape[2], volt_ref.shape[3]
    per_half = FINE // halves
    run = table_ref.shape[1] // 2
    hop = GROUP * FINE
    wide_ref[...] = jnp.broadcast_to(gain_ref[...][:, :, :, None, :], wide_ref.shape)

    def one(channel, pair, inside):
        sets = []
        for group in range(2):
            start = (2 * pair + group) * hop
            columns = []
            for part in range(2):
                if inside:
                    columns.append(volt_ref[part, channel, :, pl.ds(pl.multiple_of(start, LANES), run)])
                else:
                    stop = min(start + run, samples)
                    columns.append(volt_ref[part, channel, :, start:stop])
                    if start + run > stop:
                        columns.append(jnp.zeros((inputs, start + run - stop), volt_ref.dtype))
            sets.append(jnp.concatenate(columns, axis=1))
        lines = jnp.concatenate(sets, axis=0)
        sums = lax.dot_general(
            table_ref[...], lines, (((1,), (1,)), ((), ())), preferred_element_type=jnp.float32
        )
        sums = sums.reshape(FINE, 2, GROUP, 2 * inputs)
        raw_real = jnp.concatenate([sums[:, 0, :, :inputs], sums[:, 0, :, inputs:]], axis=1)
        raw_imag = jnp.concatenate([sums[:, 1, :, :inputs], sums[:, 1, :, inputs:]], axis=1)
        gain_real, gain_imag = wide_ref[0, channel], wide_ref[1, channel]
        real = (raw_real * gain_real - raw_imag * gain_imag).astype(jnp.bfloat16)
        imag = (raw_real * gain_imag + raw_imag * gain_real).astype(jnp.bfloat16)
        for half in range(halves):
            start = half * per_half
            for out, size, first in zip(outs, chunks, firsts):
                if not inside and pair < first:
                    start += size
                    continue
                at = 2 * GROUP * (pair - first)
                frames = pl.ds(pl.multiple_of(at, 2 * GROUP) if inside else at, 2 * GROUP)
                out[channel * halves + half, :, 0, frames, :] = real[start : start + size]
                out[channel * halves + half, :, 1, frames, :] = imag[start : start + size]
                start += size

    whole = min(pairs, (samples - run + hop) // (2 * hop))
    common = max(firsts)

    for channel in range(coarse):

        def loop(pair, _, channel=channel):
            one(channel, pair, True)
            return 0

        for pair in range(min(firsts), common):
            one(channel, pair, False)
        lax.fori_loop(common, whole, loop, 0, unroll=UNROLL)
        for pair in range(whole, pairs):
            one(channel, pair, False)


def filter_bank(voltages, gains, halves, chunks, first_frames, last_frame, together, waits=()):
    _, coarse, inputs, samples = voltages.shape
    table = filter_rows()
    run = table.shape[1] // 2
    ahead = run - GROUP * FINE
    block = min(samples, last_frame * FINE + ahead)
    return pl.pallas_call(
        functools.partial(
            filter_kernel,
            halves,
            chunks,
            [first // (2 * GROUP) for first in first_frames],
            last_frame // (2 * GROUP),
            together,
        ),
        out_shape=[
            jax.ShapeDtypeStruct((coarse * halves, count, 2, last_frame - first, inputs), jnp.bfloat16)
            for count, first in zip(chunks, first_frames)
        ],
        grid=(coarse // together,),
        in_specs=[
            pl.BlockSpec((2, together, inputs, block), lambda c: (0, c, 0, 0)),
            pl.BlockSpec((2, together, FINE, inputs), lambda c: (0, c, 0, 0)),
            pl.BlockSpec(table.shape, lambda c: (0, 0)),
        ]
        + [pl.BlockSpec(memory_space=pl.ANY)] * len(waits),
        out_specs=[
            pl.BlockSpec((together * halves, count, 2, last_frame - first, inputs), lambda c: (c, 0, 0, 0, 0))
            for count, first in zip(chunks, first_frames)
        ],
        scratch_shapes=[pltpu.VMEM((2, together, FINE, 2 * GROUP, inputs), jnp.float32)],
        compiler_params=pltpu.CompilerParams(vmem_limit_bytes=VMEM),
        cost_estimate=pl.CostEstimate(
            flops=4 * table.size * inputs * last_frame // GROUP * coarse,
            bytes_accessed=16 * coarse * inputs * last_frame * FINE,
            transcendentals=0,
        ),
        name="filter_bank",
    )(voltages, gains, jnp.asarray(table), *waits)


def gate(released, waits):
    def nothing(*_):
        pass

    anywhere = pl.BlockSpec(memory_space=pl.ANY)
    return pl.pallas_call(
        nothing,
        out_shape=[jax.ShapeDtypeStruct(array.shape, array.dtype) for array in released],
        in_specs=[anywhere] * (len(released) + len(waits)),
        out_specs=[anywhere] * len(released),
        input_output_aliases={index: index for index in range(len(released))},
        compiler_params=pltpu.CompilerParams(vmem_limit_bytes=VMEM),
        cost_estimate=pl.CostEstimate(flops=0, bytes_accessed=0, transcendentals=0),
        name="gate",
    )(*released, *waits)


def correlate_kernel(pieces, tile, scale, added, whole, where_ref, *rest):
    blocks = rest[:pieces]
    added_ref = rest[pieces] if added else None
    channel = pl.program_id(0)
    out_ref, rows_ref = rest[-2:]
    inputs = blocks[0].shape[4]
    row_count, total = out_ref.shape[1:]
    depth = rows_ref.shape[1]
    per_tile = tile // inputs
    row_tiles, column_tiles = row_count // tile, total // tile

    def columns_of(position):
        sources = [position * per_tile + index for index in range(per_tile)]
        parts = [
            jnp.concatenate([block[source, 0, part] for source in sources], axis=1)
            for part in range(2)
            for block in blocks
        ]
        return jnp.concatenate(parts, axis=0)

    first_tile = where_ref[0] * row_tiles
    unit = (
        lax.broadcasted_iota(jnp.int32, (tile, tile), 0)
        == lax.broadcasted_iota(jnp.int32, (tile, tile), 1)
    )
    unit = jnp.where(unit, 1.0, 0.0).astype(jnp.bfloat16)
    for row in range(row_tiles):
        turned = columns_of(first_tile + row).T
        imag_at = slice(row * tile, (row + 1) * tile)
        real_at = slice(row_count + row * tile, row_count + (row + 1) * tile)
        rows_ref[real_at, :] = turned
        rows_ref[imag_at, : depth // 2] = turned[:, depth // 2 :]
        rows_ref[imag_at, depth // 2 :] = -turned[:, : depth // 2]

    def product(start, size, column):
        left = rows_ref[pl.ds(pl.multiple_of(start, tile), size), :]
        return jnp.dot(left, columns_of(column), preferred_element_type=jnp.float32)

    def store(at, column_at, sums):
        if added:
            sums = sums + added_ref[channel, at, column_at]
        out_ref[channel if whole else 0, at, column_at] = (sums * scale if scale != 1.0 else sums).astype(out_ref.dtype)

    before = first_tile > 0
    start = jnp.where(before, 0, row_count)
    first_column = jnp.where(before, 0, row_tiles)
    width = total - row_count
    right = jnp.concatenate([columns_of(first_column + index) for index in range(width // tile)], axis=1)
    column_at = pl.ds(pl.multiple_of(first_column * tile, tile), width)
    left = rows_ref[pl.ds(pl.multiple_of(start, tile), row_count), :]
    store(slice(0, row_count), column_at, jnp.dot(left, right, preferred_element_type=jnp.float32))
    upper = lax.broadcasted_iota(jnp.int32, (tile, tile), 0) <= lax.broadcasted_iota(jnp.int32, (tile, tile), 1)
    column_at = pl.ds(pl.multiple_of(first_tile * tile, tile), tile)
    sums = product(0, 3 * tile, first_tile)
    store(slice(0, tile), column_at, jnp.where(upper, sums[2 * tile :], sums[:tile]))
    store(slice(tile, row_count), column_at, sums[tile : 2 * tile])
    column_at = pl.ds(pl.multiple_of((first_tile + 1) * tile, tile), tile)
    sums = product(tile, 3 * tile, first_tile + 1)
    store(slice(0, tile), column_at, sums[tile : 2 * tile])
    store(slice(tile, row_count), column_at, jnp.where(upper, sums[2 * tile :], sums[:tile]))


def correlate(pieces, where, held, first, count, channels, row_count, total, tile, scale, added=None, dtype=jnp.bfloat16):
    sources, _, _, _, inputs = pieces[0][0].shape
    depth = 2 * sum(array.shape[3] for array, _ in pieces)
    operands = [array for array, _ in pieces]
    in_specs = [
        pl.BlockSpec((sources, 1, 2, array.shape[3], inputs), lambda q, w, start=start: (0, start + q, 0, 0, 0))
        for array, start in pieces
    ]
    if added is not None:
        operands.append(added)
        in_specs.append(pl.BlockSpec(memory_space=pltpu.VMEM))
    whole = dtype == jnp.float32
    aliases = {}
    if held is not None:
        aliases = {1 + len(operands): 0}
        operands.append(held)
        in_specs.append(pl.BlockSpec(memory_space=pl.ANY))
    return pl.pallas_call(
        functools.partial(correlate_kernel, len(pieces), tile, scale, added is not None, whole),
        out_shape=jax.ShapeDtypeStruct((channels, row_count, total), dtype),
        grid_spec=pltpu.PrefetchScalarGridSpec(
            num_scalar_prefetch=1,
            grid=(count,),
            in_specs=in_specs,
            out_specs=pl.BlockSpec(memory_space=pltpu.VMEM)
            if whole
            else pl.BlockSpec((1, row_count, total), lambda q, w: (first + q, 0, 0)),
            scratch_shapes=[pltpu.VMEM((2 * row_count, depth), jnp.bfloat16)],
        ),
        input_output_aliases=aliases,
        compiler_params=pltpu.CompilerParams(vmem_limit_bytes=VMEM * 5 // 8 if whole or added is not None else VMEM),
        cost_estimate=pl.CostEstimate(
            flops=count * 8 * row_count * total * depth,
            bytes_accessed=count * 16 * total * depth,
            transcendentals=0,
        ),
        name="correlate",
    )(where, *operands)


def chunk_sizes(channels):
    cuts = sorted({0} | {max(1, channels * part // 16) for part in PARTS})
    return [stop - start for start, stop in zip(cuts, cuts[1:])]


def local_kernels(count, spans, voltages, gains):
    coarse, inputs, samples = voltages.shape[1:]
    frames = samples // FINE
    halves = count // coarse
    channels = FINE // halves
    chunks = chunk_sizes(channels)
    total = count * inputs
    row_count = total // spans
    early = max(2 * GROUP, frames * EARLY // 16 // (2 * GROUP) * (2 * GROUP))
    scale = 1.0 / (spans * frames)
    where = jnp.stack([lax.axis_index("span")]).astype(jnp.int32)
    gains = jnp.swapaxes(gains, 2, 3)

    def across(array):
        return lax.all_to_all(array, "inp", split_axis=0, concat_axis=0, tiled=True)

    def other_spans(array):
        return [
            lax.ppermute(array, "span", [(i, i ^ other) for i in range(spans)]) for other in range(1, spans)
        ]

    ahead = chunks[:-1] if len(chunks) > 1 else chunks
    begins = [early] * len(ahead) + [0] * (len(chunks) - len(ahead))
    outgoing = filter_bank(voltages, gains, halves, [sum(ahead)], [0], early, TOGETHER if coarse % TOGETHER == 0 else 1)
    outgoing = list(outgoing)
    outgoing += list(filter_bank(voltages, gains, halves, chunks, begins, frames, 1, outgoing))
    turned = across(outgoing[0])
    outgoing[1] = gate([outgoing[1]], [turned])[0]
    first_frames = [turned] + other_spans(turned)
    held, first = None, 0
    for index, size in enumerate(chunks):
        turned = across(outgoing[1 + index])
        if held is not None:
            turned, held = gate([turned, held], [])
        others = other_spans(turned)
        pieces = [(array, first) for array in first_frames] if begins[index] else []
        added = None
        if pieces:
            pieces += [(turned, 0)] + [(array, 0) for array in others]
        else:
            added = correlate(
                [(turned, 0)], where, None, 0, size, size, row_count, total, 2 * LANES, 1.0, None, jnp.float32
            )
            pieces = [(array, 0) for array in others]
        held = correlate(
            pieces, where, held, first, size, channels, row_count, total, 2 * LANES, scale, added
        )
        first += size
    return held


def power_of_two(number):
    return number > 0 and number & (number - 1) == 0


def solution(mesh):
    count, spans = mesh.shape["inp"], mesh.shape["span"]

    def local(voltages, gains):
        coarse, inputs, samples = voltages.shape[1:]
        fits = (
            power_of_two(count)
            and power_of_two(spans)
            and count % coarse == 0
            and power_of_two(count // coarse)
            and FINE % (count // coarse) == 0
            and (FINE // (count // coarse)) % 8 == 0
            and inputs == LANES
            and spans > 1
            and samples % (2 * GROUP * FINE) == 0
            and samples >= 8 * GROUP * FINE
            and count * inputs // spans == 4 * LANES
        )
        if fits:
            return local_kernels(count, spans, voltages, gains)
        return local_plain(voltages, gains)

    placed = (P(None, "beam", "inp", "span"), P(None, "beam", "inp", None))
    return jax.shard_map(
        local,
        mesh=mesh,
        in_specs=placed,
        out_specs=P(("beam", "inp"), "span", None),
        check_vma=False,
    )
```

```python
import functools
import math

import jax
import jax.numpy as jnp
import ml_dtypes
import numpy as np
from jax import lax
from jax.experimental import pallas as pl
from jax.experimental.pallas import tpu as pltpu
from jax.sharding import PartitionSpec as P

FINE = 32
TAPS = 4
LANES = 128
GROUP = 8
VMEM = 64 * 1024 * 1024 - 64 * 1024
UNROLL = 7
TOGETHER = 2
EARLY = 1
PARTS = (14, 16)


def prototype(tap_count, fine_count):
    length = tap_count * fine_count
    offsets = jnp.arange(length).astype(jnp.float32)
    shifted = (offsets - length / 2 + 0.5) / fine_count
    taper = 0.5 - 0.5 * jnp.cos(2.0 * math.pi * (offsets + 0.5) / length)
    window = jnp.sinc(shifted) * taper
    window = window / jnp.sqrt(jnp.sum(window * window))
    return window.reshape(tap_count, fine_count)


def kernels(window, fine_count):
    points = jnp.arange(fine_count)
    phase_steps = points[:, None] * points[None, :] % fine_count
    angles = 2.0 * math.pi * phase_steps.astype(jnp.float32) / fine_count
    cosine = jnp.cos(angles)
    sine_part = jnp.sin(angles)
    result = []
    for tap_index in range(window.shape[0]):
        weights = window[tap_index][:, None]
        hcos = weights * cosine
        hsin = weights * sine_part
        result.append(jnp.stack([jnp.stack([hcos, -hsin]), jnp.stack([hsin, hcos])]))
    return jnp.stack(result)


def packed_rows(left_rows, right_rows, left_all, row_start):
    real_sums = jnp.einsum("cif,cjf->cij", left_rows, left_all, preferred_element_type=jnp.float32)
    imag_sums = jnp.einsum("cif,cjf->cij", right_rows, left_all, preferred_element_type=jnp.float32)
    row_index = row_start + jnp.arange(left_rows.shape[1])
    col_index = jnp.arange(left_all.shape[1])
    upper = row_index[:, None] <= col_index[None, :]
    return jnp.where(upper[None], real_sums, imag_sums)


def local_plain(voltages, gains):
    coarse = voltages.shape[1]
    local_inputs = voltages.shape[2]
    samples = voltages.shape[3]
    frames = samples // FINE
    window = prototype(TAPS, FINE)
    filters = kernels(window, FINE)
    filter_table = jnp.transpose(filters, (1, 0, 3, 2, 4))
    filter_high = filter_table.astype(jnp.bfloat16)
    filter_low = (filter_table - filter_high.astype(jnp.float32)).astype(jnp.bfloat16)
    padded = jnp.pad(voltages, ((0, 0), (0, 0), (0, 0), (0, (TAPS - 1) * FINE)))
    stacked = jnp.stack(
        [padded[..., tap_index * FINE : tap_index * FINE + samples] for tap_index in range(TAPS)],
        axis=1,
    )
    stacked = stacked.reshape(2, TAPS, coarse, local_inputs, frames, FINE)
    spectra = jnp.einsum(
        "atcnmp,atpbk->bcknm", stacked, filter_high, preferred_element_type=jnp.float32
    )
    spectra = spectra + jnp.einsum(
        "atcnmp,atpbk->bcknm", stacked, filter_low, preferred_element_type=jnp.float32
    )
    gain_real = jnp.swapaxes(gains[0], 1, 2)[:, :, :, None]
    gain_imag = jnp.swapaxes(gains[1], 1, 2)[:, :, :, None]
    real_part = spectra[0] * gain_real - spectra[1] * gain_imag
    imag_part = spectra[0] * gain_imag + spectra[1] * gain_real
    outgoing = jnp.stack([real_part, imag_part]).astype(jnp.bfloat16)
    outgoing = outgoing.reshape(2, coarse * FINE, local_inputs, frames)
    turned = lax.all_to_all(outgoing, "inp", split_axis=1, concat_axis=2, tiled=True)
    inputs = turned.shape[2]
    span_count = lax.axis_size("span")
    row_count = inputs // span_count
    frame_scale = 1.0 / (span_count * frames)
    row_start = lax.axis_index("span") * row_count
    frame_piece = lax.all_gather(turned, "span", axis=3, tiled=True)
    left_all = jnp.concatenate([frame_piece[0], frame_piece[1]], axis=-1)
    own_rows = lax.dynamic_slice_in_dim(frame_piece, row_start, row_count, 2)
    left_rows = jnp.concatenate([own_rows[0], own_rows[1]], axis=-1)
    right_rows = jnp.concatenate([own_rows[1], -own_rows[0]], axis=-1)
    summed = packed_rows(left_rows, right_rows, left_all, row_start) * frame_scale
    return summed.astype(jnp.bfloat16)


def filter_rows():
    length = TAPS * FINE
    run = -(-(GROUP * FINE + length - FINE) // LANES) * LANES
    offsets = np.arange(length)
    window = np.sinc((offsets - length / 2 + 0.5) / FINE)
    window = window * (0.5 - 0.5 * np.cos(2.0 * np.pi * (offsets + 0.5) / length))
    window = window / np.sqrt(np.sum(window * window))
    angles = 2.0 * np.pi * (offsets[None, :] * np.arange(FINE)[:, None] % FINE) / FINE
    hcos = window * np.cos(angles)
    hsin = window * np.sin(angles)
    table = np.zeros((FINE, 2, GROUP, 2, run))
    for frame in range(GROUP):
        at = slice(frame * FINE, frame * FINE + length)
        table[:, 0, frame, 0, at] = hcos
        table[:, 0, frame, 1, at] = hsin
        table[:, 1, frame, 0, at] = -hsin
        table[:, 1, frame, 1, at] = hcos
    return table.reshape(-1, 2 * run).astype(ml_dtypes.bfloat16)


def filter_kernel(halves, chunks, firsts, pairs, coarse, volt_ref, gain_ref, table_ref, *rest):
    outs, wide_ref = rest[-1 - len(chunks) : -1], rest[-1]
    inputs, samples = volt_ref.shape[2], volt_ref.shape[3]
    per_half = FINE // halves
    run = table_ref.shape[1] // 2
    hop = GROUP * FINE
    wide_ref[...] = jnp.broadcast_to(gain_ref[...][:, :, :, None, :], wide_ref.shape)

    def one(channel, pair, inside):
        sets = []
        for group in range(2):
            start = (2 * pair + group) * hop
            columns = []
            for part in range(2):
                if inside:
                    columns.append(volt_ref[part, channel, :, pl.ds(pl.multiple_of(start, LANES), run)])
                else:
                    stop = min(start + run, samples)
                    columns.append(volt_ref[part, channel, :, start:stop])
                    if start + run > stop:
                        columns.append(jnp.zeros((inputs, start + run - stop), volt_ref.dtype))
            sets.append(jnp.concatenate(columns, axis=1))
        lines = jnp.concatenate(sets, axis=0)
        sums = lax.dot_general(
            table_ref[...], lines, (((1,), (1,)), ((), ())), preferred_element_type=jnp.float32
        )
        sums = sums.reshape(FINE, 2, GROUP, 2 * inputs)
        raw_real = jnp.concatenate([sums[:, 0, :, :inputs], sums[:, 0, :, inputs:]], axis=1)
        raw_imag = jnp.concatenate([sums[:, 1, :, :inputs], sums[:, 1, :, inputs:]], axis=1)
        gain_real, gain_imag = wide_ref[0, channel], wide_ref[1, channel]
        real = (raw_real * gain_real - raw_imag * gain_imag).astype(jnp.bfloat16)
        imag = (raw_real * gain_imag + raw_imag * gain_real).astype(jnp.bfloat16)
        for half in range(halves):
            start = half * per_half
            for out, size, first in zip(outs, chunks, firsts):
                if not inside and pair < first:
                    start += size
                    continue
                at = 2 * GROUP * (pair - first)
                frames = pl.ds(pl.multiple_of(at, 2 * GROUP) if inside else at, 2 * GROUP)
                out[channel * halves + half, :, 0, frames, :] = real[start : start + size]
                out[channel * halves + half, :, 1, frames, :] = imag[start : start + size]
                start += size

    whole = min(pairs, (samples - run + hop) // (2 * hop))
    common = max(firsts)

    for channel in range(coarse):

        def loop(pair, _, channel=channel):
            one(channel, pair, True)
            return 0

        for pair in range(min(firsts), common):
            one(channel, pair, False)
        lax.fori_loop(common, whole, loop, 0, unroll=UNROLL)
        for pair in range(whole, pairs):
            one(channel, pair, False)


def filter_bank(voltages, gains, halves, chunks, first_frames, last_frame, together, waits=()):
    _, coarse, inputs, samples = voltages.shape
    table = filter_rows()
    run = table.shape[1] // 2
    ahead = run - GROUP * FINE
    block = min(samples, last_frame * FINE + ahead)
    return pl.pallas_call(
        functools.partial(
            filter_kernel,
            halves,
            chunks,
            [first // (2 * GROUP) for first in first_frames],
            last_frame // (2 * GROUP),
            together,
        ),
        out_shape=[
            jax.ShapeDtypeStruct((coarse * halves, count, 2, last_frame - first, inputs), jnp.bfloat16)
            for count, first in zip(chunks, first_frames)
        ],
        grid=(coarse // together,),
        in_specs=[
            pl.BlockSpec((2, together, inputs, block), lambda c: (0, c, 0, 0)),
            pl.BlockSpec((2, together, FINE, inputs), lambda c: (0, c, 0, 0)),
            pl.BlockSpec(table.shape, lambda c: (0, 0)),
        ]
        + [pl.BlockSpec(memory_space=pl.ANY)] * len(waits),
        out_specs=[
            pl.BlockSpec((together * halves, count, 2, last_frame - first, inputs), lambda c: (c, 0, 0, 0, 0))
            for count, first in zip(chunks, first_frames)
        ],
        scratch_shapes=[pltpu.VMEM((2, together, FINE, 2 * GROUP, inputs), jnp.float32)],
        compiler_params=pltpu.CompilerParams(vmem_limit_bytes=VMEM),
        cost_estimate=pl.CostEstimate(
            flops=4 * table.size * inputs * last_frame // GROUP * coarse,
            bytes_accessed=16 * coarse * inputs * last_frame * FINE,
            transcendentals=0,
        ),
        name="filter_bank",
    )(voltages, gains, jnp.asarray(table), *waits)


def gate(released, waits):
    def nothing(*_):
        pass

    anywhere = pl.BlockSpec(memory_space=pl.ANY)
    return pl.pallas_call(
        nothing,
        out_shape=[jax.ShapeDtypeStruct(array.shape, array.dtype) for array in released],
        in_specs=[anywhere] * (len(released) + len(waits)),
        out_specs=[anywhere] * len(released),
        input_output_aliases={index: index for index in range(len(released))},
        compiler_params=pltpu.CompilerParams(vmem_limit_bytes=VMEM),
        cost_estimate=pl.CostEstimate(flops=0, bytes_accessed=0, transcendentals=0),
        name="gate",
    )(*released, *waits)


def correlate_kernel(pieces, tile, scale, added, whole, where_ref, *rest):
    blocks = rest[:pieces]
    added_ref = rest[pieces] if added else None
    channel = pl.program_id(0)
    out_ref, rows_ref = rest[-2:]
    inputs = blocks[0].shape[4]
    row_count, total = out_ref.shape[1:]
    depth = rows_ref.shape[1]
    per_tile = tile // inputs
    row_tiles, column_tiles = row_count // tile, total // tile

    def columns_of(position):
        sources = [position * per_tile + index for index in range(per_tile)]
        parts = [
            jnp.concatenate([block[source, channel if added else 0, part] for source in sources], axis=1)
            for part in range(2)
            for block in blocks
        ]
        return jnp.concatenate(parts, axis=0)

    first_tile = where_ref[0] * row_tiles
    unit = (
        lax.broadcasted_iota(jnp.int32, (tile, tile), 0)
        == lax.broadcasted_iota(jnp.int32, (tile, tile), 1)
    )
    unit = jnp.where(unit, 1.0, 0.0).astype(jnp.bfloat16)
    for row in range(row_tiles):
        turned = columns_of(first_tile + row).T
        imag_at = slice(row * tile, (row + 1) * tile)
        real_at = slice(row_count + row * tile, row_count + (row + 1) * tile)
        rows_ref[real_at, :] = turned
        rows_ref[imag_at, : depth // 2] = turned[:, depth // 2 :]
        rows_ref[imag_at, depth // 2 :] = -turned[:, : depth // 2]

    def product(start, size, column):
        left = rows_ref[pl.ds(pl.multiple_of(start, tile), size), :]
        return jnp.dot(left, columns_of(column), preferred_element_type=jnp.float32)

    def store(at, column_at, sums):
        if added:
            sums = sums + added_ref[channel, at, column_at]
        out_ref[channel if whole else 0, at, column_at] = (sums * scale if scale != 1.0 else sums).astype(out_ref.dtype)

    before = first_tile > 0
    start = jnp.where(before, 0, row_count)
    first_column = jnp.where(before, 0, row_tiles)
    width = total - row_count
    right = jnp.concatenate([columns_of(first_column + index) for index in range(width // tile)], axis=1)
    column_at = pl.ds(pl.multiple_of(first_column * tile, tile), width)
    left = rows_ref[pl.ds(pl.multiple_of(start, tile), row_count), :]
    store(slice(0, row_count), column_at, jnp.dot(left, right, preferred_element_type=jnp.float32))
    upper = lax.broadcasted_iota(jnp.int32, (tile, tile), 0) <= lax.broadcasted_iota(jnp.int32, (tile, tile), 1)
    column_at = pl.ds(pl.multiple_of(first_tile * tile, tile), tile)
    sums = product(0, 3 * tile, first_tile)
    store(slice(0, tile), column_at, jnp.where(upper, sums[2 * tile :], sums[:tile]))
    store(slice(tile, row_count), column_at, sums[tile : 2 * tile])
    column_at = pl.ds(pl.multiple_of((first_tile + 1) * tile, tile), tile)
    sums = product(tile, 3 * tile, first_tile + 1)
    store(slice(0, tile), column_at, sums[tile : 2 * tile])
    store(slice(tile, row_count), column_at, jnp.where(upper, sums[2 * tile :], sums[:tile]))


def correlate(pieces, where, held, first, count, channels, row_count, total, tile, scale, added=None, dtype=jnp.bfloat16):
    sources, _, _, _, inputs = pieces[0][0].shape
    depth = 2 * sum(array.shape[3] for array, _ in pieces)
    operands = [array for array, _ in pieces]
    in_specs = [
        pl.BlockSpec((sources, 1, 2, array.shape[3], inputs), lambda q, w, start=start: (0, start + q, 0, 0, 0))
        for array, start in pieces
    ]
    if added is not None:
        in_specs = [pl.BlockSpec(memory_space=pltpu.VMEM) for _ in pieces]
        operands.append(added)
        in_specs.append(pl.BlockSpec(memory_space=pltpu.VMEM))
    whole = dtype == jnp.float32
    aliases = {}
    if held is not None:
        aliases = {1 + len(operands): 0}
        operands.append(held)
        in_specs.append(pl.BlockSpec(memory_space=pl.ANY))
    return pl.pallas_call(
        functools.partial(correlate_kernel, len(pieces), tile, scale, added is not None, whole),
        out_shape=jax.ShapeDtypeStruct((channels, row_count, total), dtype),
        grid_spec=pltpu.PrefetchScalarGridSpec(
            num_scalar_prefetch=1,
            grid=(count,),
            in_specs=in_specs,
            out_specs=pl.BlockSpec(memory_space=pltpu.VMEM)
            if whole
            else pl.BlockSpec((1, row_count, total), lambda q, w: (first + q, 0, 0)),
            scratch_shapes=[pltpu.VMEM((2 * row_count, depth), jnp.bfloat16)],
        ),
        input_output_aliases=aliases,
        compiler_params=pltpu.CompilerParams(vmem_limit_bytes=VMEM * 5 // 8 if whole or added is not None else VMEM),
        cost_estimate=pl.CostEstimate(
            flops=count * 8 * row_count * total * depth,
            bytes_accessed=count * 16 * total * depth,
            transcendentals=0,
        ),
        name="correlate",
    )(where, *operands)


def chunk_sizes(channels):
    cuts = sorted({0} | {max(1, channels * part // 16) for part in PARTS})
    return [stop - start for start, stop in zip(cuts, cuts[1:])]


def local_kernels(count, spans, voltages, gains):
    coarse, inputs, samples = voltages.shape[1:]
    frames = samples // FINE
    halves = count // coarse
    channels = FINE // halves
    chunks = chunk_sizes(channels)
    total = count * inputs
    row_count = total // spans
    early = max(2 * GROUP, frames * EARLY // 16 // (2 * GROUP) * (2 * GROUP))
    scale = 1.0 / (spans * frames)
    where = jnp.stack([lax.axis_index("span")]).astype(jnp.int32)
    gains = jnp.swapaxes(gains, 2, 3)

    def across(array):
        return lax.all_to_all(array, "inp", split_axis=0, concat_axis=0, tiled=True)

    def other_spans(array):
        return [
            lax.ppermute(array, "span", [(i, i ^ other) for i in range(spans)]) for other in range(1, spans)
        ]

    ahead = chunks[:-1] if len(chunks) > 1 else chunks
    begins = [early] * len(ahead) + [0] * (len(chunks) - len(ahead))
    outgoing = filter_bank(voltages, gains, halves, [sum(ahead)], [0], early, TOGETHER if coarse % TOGETHER == 0 else 1)
    outgoing = list(outgoing)
    outgoing += list(filter_bank(voltages, gains, halves, chunks, begins, frames, 1, outgoing))
    turned = across(outgoing[0])
    outgoing[1] = gate([outgoing[1]], [turned])[0]
    first_frames = [turned] + other_spans(turned)
    held, first = None, 0
    for index, size in enumerate(chunks):
        turned = across(outgoing[1 + index])
        if held is not None:
            turned, held = gate([turned, held], [])
        others = other_spans(turned)
        pieces = [(array, first) for array in first_frames] if begins[index] else []
        added = None
        if pieces:
            pieces += [(turned, 0)] + [(array, 0) for array in others]
        else:
            added = correlate(
                [(turned, 0)], where, None, 0, size, size, row_count, total, 2 * LANES, 1.0, None, jnp.float32
            )
            pieces = [(array, 0) for array in others]
        held = correlate(
            pieces, where, held, first, size, channels, row_count, total, 2 * LANES, scale, added
        )
        first += size
    return held


def power_of_two(number):
    return number > 0 and number & (number - 1) == 0


def solution(mesh):
    count, spans = mesh.shape["inp"], mesh.shape["span"]

    def local(voltages, gains):
        coarse, inputs, samples = voltages.shape[1:]
        fits = (
            power_of_two(count)
            and power_of_two(spans)
            and count % coarse == 0
            and power_of_two(count // coarse)
            and FINE % (count // coarse) == 0
            and (FINE // (count // coarse)) % 8 == 0
            and inputs == LANES
            and spans > 1
            and samples % (2 * GROUP * FINE) == 0
            and samples >= 8 * GROUP * FINE
            and count * inputs // spans == 4 * LANES
        )
        if fits:
            return local_kernels(count, spans, voltages, gains)
        return local_plain(voltages, gains)

    placed = (P(None, "beam", "inp", "span"), P(None, "beam", "inp", None))
    return jax.shard_map(
        local,
        mesh=mesh,
        in_specs=placed,
        out_specs=P(("beam", "inp"), "span", None),
        check_vma=False,
    )
```
